128 devices in a mesh: ctx: 32 (over x, z_lo, y), chan: 4 (over z_hi, core).
Axes of the slice: x: 4, y: 4, z: 4 (z_hi: 2, z_lo: 2; z = z_hi * 2 + z_lo), core: 2. Of those that a mesh axis runs over, the one named last changes fastest.
Arguments:
- queries: bfloat16 [4096, 4096], P('ctx', 'chan'), may hold values from -8 to 8
- key_rows: bfloat16 [4096, 4096], P('ctx', 'chan'), may hold values from -8 to 8
- value_rows: bfloat16 [4096, 4096], P('ctx', 'chan'), may hold values from -16 to 16
- gate_in: bfloat16 [4096, 4096], P('ctx', 'chan'), may hold values from -6 to 6
- gate_out: bfloat16 [4096, 4096], P('ctx', 'chan'), may hold values from -6 to 6
- kernel_taps: float32 [512, 7], P('chan'), may hold values from -2 to 2
- norm_gain: float32 [4096], P('chan'), may hold values from 0.1 to 1.9
- cotangent: bfloat16 [4096, 4096], P('ctx', 'chan'), may hold values from -6 to 6
Outputs:
- mixed: bfloat16 [4096, 4096], P('ctx', 'chan')
- grad_queries: bfloat16 [4096, 4096], P('ctx', 'chan')
- grad_keys: bfloat16 [4096, 4096], P('ctx', 'chan')
- grad_values: bfloat16 [4096, 4096], P('ctx', 'chan')
- grad_gate_in: bfloat16 [4096, 4096], P('ctx', 'chan')
- grad_gate_out: bfloat16 [4096, 4096], P('ctx', 'chan')
- grad_filter: float32 [512, 7], P('chan')
- grad_gain: float32 [4096], P('chan')
The draws below stay inside these ranges and needn't reach their ends.
All inputs are finite; a program needn't handle non-finite values.
Results may differ from the reference program's by a relative error of at most 0.015.
Values may be sent and summed in bfloat16 or wider, within the bound.
A program may use at most 128 MiB of HBM per device.

```python
import jax
import jax.numpy as jnp
from jax import lax

HEADS = 32
HEAD = 128
GROUPS = 512
FILT = 7
TOKENS = 4096
WIDTH = 4096
GROUP_SIZE = 8


def draw_queries(key, part):
    shape = (TOKENS, HEADS * HEAD)
    values = jnp.clip(jax.random.normal(jax.random.fold_in(key, 1), shape, jnp.float32), -4.0, 4.0)
    return values.astype(jnp.bfloat16)


def draw_key_rows(key, part):
    shape = (TOKENS, HEADS * HEAD)
    values = jnp.clip(jax.random.normal(jax.random.fold_in(key, 2), shape, jnp.float32), -4.0, 4.0)
    return values.astype(jnp.bfloat16)


def draw_value_rows(key, part):
    shape = (TOKENS, HEADS * HEAD)
    column = jnp.arange(HEADS * HEAD, dtype=jnp.float32) / (HEADS * HEAD)
    spread = jnp.exp(jax.random.uniform(jax.random.fold_in(key, 4), (HEADS * HEAD,), jnp.float32, 0.0, 1.2))
    base = jnp.clip(jax.random.normal(jax.random.fold_in(key, 3), shape, jnp.float32), -4.0, 4.0)
    trend = jnp.exp(1.1 * column)
    return jnp.clip(base * (trend * spread)[None, :], -16.0, 16.0).astype(jnp.bfloat16)


def steps_of(rng, dims, split, smallest, largest):
    def one(axis_at, parts):
        heights = jax.random.uniform(jax.random.fold_in(jax.random.fold_in(rng, 6), axis_at), (parts,), jnp.float32, smallest / len(split), largest / len(split))
        return jnp.repeat(jnp.exp(heights), dims[axis_at] // parts).reshape((-1,) + (1,) * (len(dims) - axis_at - 1))

    loudness = one(*split[0])
    for cut in split[1:]:
        loudness = loudness * one(*cut)
    return loudness


def scatter_about(rng, extent, scale, bound, split=(), kind=jnp.bfloat16):
    values = scale * jax.random.normal(rng, extent, jnp.float32)
    if split:
        values = values * steps_of(rng, extent, split, -0.22, 0.18)
    return jnp.clip(values, -bound, bound).astype(kind)


def setup_inputs(seed: int = 0) -> dict:
    key_list = jax.random.split(jax.random.key(seed), 9)
    queries = draw_queries(jax.random.fold_in(key_list[8], 71), 0)
    key_rows = draw_key_rows(jax.random.fold_in(key_list[8], 71), 0)
    value_rows = draw_value_rows(jax.random.fold_in(key_list[8], 71), 0)
    gate_in = scatter_about(key_list[3], (TOKENS, WIDTH), 1.0, 6.0, ((0, 32), (1, 4)))
    gate_out = scatter_about(key_list[4], (TOKENS, WIDTH), 1.0, 6.0, ((0, 32), (1, 4)))
    kernel_taps = scatter_about(key_list[5], (GROUPS, FILT), 0.4, 2.0, ((0, 4),), jnp.float32)
    norm_gain = jnp.clip(1.0 + 0.18 * jax.random.normal(key_list[6], (WIDTH,), jnp.float32), 0.1, 1.9)
    cotangent = scatter_about(key_list[7], (TOKENS, WIDTH), 1.0, 6.0, ((0, 32), (1, 4)))
    return dict(queries=queries, key_rows=key_rows, value_rows=value_rows, gate_in=gate_in, gate_out=gate_out, kernel_taps=kernel_taps, norm_gain=norm_gain, cotangent=cotangent)


EPS = 1e-06
NEG = -1e+30

def causal_scores(q_head, k_head):
    scores = jnp.dot(q_head, k_head.T, precision=lax.Precision.HIGHEST) * HEAD ** (-0.5)
    rows_pos = jnp.arange(TOKENS, dtype=jnp.int32)
    allowed = rows_pos[:, None] >= rows_pos[None, :]
    return jnp.where(allowed, scores, NEG)

def round_trip(values):
    return lax.optimization_barrier(values.astype(jnp.bfloat16)).astype(jnp.float32)

def head_forward(blocks):
    q_head, k_head, v_head = blocks
    scores = causal_scores(q_head, k_head)
    row_max = lax.optimization_barrier(jnp.max(scores, axis=1, keepdims=True))
    lse = row_max[:, 0] + jnp.log(lax.optimization_barrier(jnp.sum(jnp.exp(scores - row_max), axis=1)))
    weights = round_trip(jnp.exp(scores - lse[:, None]))
    output = jnp.dot(weights, v_head, precision=lax.Precision.HIGHEST)
    return (output.astype(jnp.bfloat16), lse)

def head_backward(blocks):
    q_head, k_head, v_head, lse, d_out, delta = blocks
    scores = causal_scores(q_head, k_head)
    weights = jnp.exp(scores - lse[:, None])
    d_probs = jnp.dot(d_out, v_head.T, precision=lax.Precision.HIGHEST)
    d_scores = round_trip(weights * (d_probs - delta[:, None]))
    scale = HEAD ** (-0.5)
    grad_q = (jnp.dot(d_scores, k_head, precision=lax.Precision.HIGHEST) * scale).astype(jnp.bfloat16)
    grad_k = (jnp.dot(d_scores.T, q_head, precision=lax.Precision.HIGHEST) * scale).astype(jnp.bfloat16)
    grad_v = jnp.dot(round_trip(weights).T, d_out, precision=lax.Precision.HIGHEST).astype(jnp.bfloat16)
    return (grad_q, grad_k, grad_v)

def split_heads(matrix):
    return matrix.astype(jnp.float32).reshape(TOKENS, HEADS, HEAD).transpose(1, 0, 2)

def join_heads(stacked):
    return stacked.transpose(1, 0, 2).reshape(TOKENS, WIDTH)

def shift_down(field, lag):
    return jnp.pad(field, ((lag, 0), (0, 0)))[:TOKENS]

def shift_up(field, lag):
    return jnp.pad(field, ((0, lag), (0, 0)))[lag:]

def reference(queries, key_rows, value_rows, gate_in, gate_out, kernel_taps, norm_gain, cotangent):
    q_heads = split_heads(queries)
    k_heads = split_heads(key_rows)
    v_heads = split_heads(value_rows)
    out_heads, lse_heads = lax.map(head_forward, (q_heads, k_heads, v_heads))
    attn = join_heads(out_heads)
    attn_wide = attn.astype(jnp.float32)
    rstd = 1.0 / jnp.sqrt(lax.optimization_barrier(jnp.sum(attn_wide * attn_wide, axis=1)) / WIDTH + EPS)
    normed = attn_wide * rstd[:, None] * norm_gain[None, :]
    gate_wide = gate_in.astype(jnp.float32)
    mixed_in = gate_wide * normed
    taps = jnp.repeat(kernel_taps, GROUP_SIZE, axis=0)
    conv_out = jnp.zeros((TOKENS, WIDTH), jnp.float32)
    for lag in range(FILT):
        conv_out = conv_out + taps[:, lag][None, :] * shift_down(mixed_in, lag)
    out_gate = gate_out.astype(jnp.float32)
    mixed = (out_gate * conv_out).astype(jnp.bfloat16)
    upstream = cotangent.astype(jnp.float32)
    grad_gate_out = (upstream * conv_out).astype(jnp.bfloat16)
    d_conv = upstream * out_gate
    columns = []
    d_mixed = jnp.zeros((TOKENS, WIDTH), jnp.float32)
    for lag in range(FILT):
        per_channel = lax.optimization_barrier(jnp.sum(d_conv * shift_down(mixed_in, lag), axis=0))
        columns.append(per_channel.reshape(GROUPS, GROUP_SIZE).sum(axis=1))
        d_mixed = d_mixed + taps[:, lag][None, :] * shift_up(d_conv, lag)
    grad_filter = jnp.stack(columns, axis=1)
    grad_gate_in = (d_mixed * normed).astype(jnp.bfloat16)
    d_normed = d_mixed * gate_wide
    grad_gain = lax.optimization_barrier(jnp.sum(d_normed * attn_wide * rstd[:, None], axis=0))
    scaled = d_normed * norm_gain[None, :]
    rowdot = lax.optimization_barrier(jnp.sum(scaled * attn_wide, axis=1))
    d_attn = (rstd[:, None] * scaled - attn_wide * (rstd ** 3 * rowdot / WIDTH)[:, None]).astype(jnp.bfloat16)
    d_heads = split_heads(d_attn)
    delta = lax.optimization_barrier(jnp.sum(d_heads * split_heads(attn), axis=2))
    grad_q, grad_k, grad_v = lax.map(head_backward, (q_heads, k_heads, v_heads, lse_heads, d_heads, delta))
    return (mixed, join_heads(grad_q), join_heads(grad_k), join_heads(grad_v), grad_gate_in, grad_gate_out, grad_filter, grad_gain)
```

```python
import functools
import math

import jax
import jax.numpy as jnp
from jax import lax
from jax.experimental import pallas as pl
from jax.experimental.pallas import tpu as pltpu
from jax.sharding import PartitionSpec as P

HEAD = 128
FILT = 7
WIDTH = 4096
EPS = 1e-06
NEG = -1e30
SCALE = HEAD ** (-0.5)
SCALE2 = SCALE * math.log2(math.e)
BLOCK = 128
CHUNK = 512
F32 = jnp.float32
BF16 = jnp.bfloat16


def dot(a, b, ca, cb, precision=None):
    return lax.dot_general(
        a, b, (((ca,), (cb,)), ((), ())), preferred_element_type=F32, precision=precision
    )


def kernel(
    q_ref, k_ref, v_ref, gi_ref, go_ref, taps_ref, gain_ref, cot_ref,
    mixed_ref, gq_ref, gk_ref, gv_ref, ggi_ref, ggo_ref, gf_ref, gg_ref,
    kvs, qs, ssrc, kvb, qb, sb, du, dz, ot, lse2, osrc, ob, stat_in, tot, hst,
    dqs, dqb, dk_acc, dv_acc, dkvs, dkvb, zx, gsrc, gin,
    kv_send, q_send, s_send, o_send, st_send, h_send, dq_send, dkv_send, g_send, rim_send,
    kv_recv, q_recv, s_recv, o_recv, st_recv, h_recv, dq_recv, dkv_recv, g_recv, rim_recv,
):
    p = lax.axis_index("ctx")
    chan = lax.axis_index("chan")
    zh, core = chan // 2, chan % 2
    x, z, y = p // 8, (p // 4) % 2, p % 4
    host = x * 4 + y
    hl0, m0 = host // 2, host % 2
    home_chan = zh * 2 + z
    r0 = m0 * 2 + core
    head0 = home_chan * 8 + hl0

    def chip(bit, e):
        return (e // 4) * 8 + bit * 4 + e % 4

    def send(src, dst, send_sem, recv_sem, p2, chan2):
        own = jnp.logical_and(p2 == p, chan2 == chan)

        @pl.when(own)
        def _():
            pltpu.make_async_copy(src, dst, recv_sem).start()

        @pl.when(jnp.logical_not(own))
        def _():
            pltpu.make_async_remote_copy(
                src_ref=src, dst_ref=dst, send_sem=send_sem, recv_sem=recv_sem,
                device_id={"ctx": p2, "chan": chan2}, device_id_type=pl.DeviceIdType.MESH,
            ).start()

    def sent(src, dst, send_sem, recv_sem, p2, chan2):
        own = jnp.logical_and(p2 == p, chan2 == chan)

        @pl.when(jnp.logical_not(own))
        def _():
            pltpu.make_async_remote_copy(
                src_ref=src, dst_ref=dst, send_sem=send_sem, recv_sem=recv_sem,
                device_id={"ctx": p2, "chan": chan2}, device_id_type=pl.DeviceIdType.MESH,
            ).wait_send()

    def arrived(buf, recv_sem):
        pltpu.make_async_copy(buf, buf, recv_sem).wait()

    def kv_plan(i):
        e, c2 = (host + i // 2) % 16, (core + i) % 2
        return kvs.at[e // 2], kvb.at[p], kv_send.at[i], kv_recv, chip(core, e), zh * 2 + c2

    own_chunk = p // 4
    own_r = jnp.minimum(own_chunk, 7 - own_chunk)
    own_slot = (own_chunk // 4) * 4 + p % 4

    def q_plan(i):
        hl = (hl0 + i) % 8
        return (
            qs.at[hl], qb.at[own_slot], q_send.at[i], q_recv,
            chip(core, hl * 2 + own_r // 2), zh * 2 + own_r % 2,
        )

    def s_plan(i):
        hl = (hl0 + i) % 8
        return (
            ssrc.at[hl], sb.at[own_slot], s_send.at[i], s_recv,
            chip(core, hl * 2 + own_r // 2), zh * 2 + own_r % 2,
        )

    def slot_home(slot):
        return jnp.where(slot < 4, r0 * 4 + slot, (7 - r0) * 4 + slot - 4)

    def o_plan(i):
        return osrc.at[i], ob.at[hl0], o_send.at[i], o_recv, slot_home(i), home_chan

    def dq_plan(i):
        return dqs.at[i], dqb.at[hl0], dq_send.at[i], dq_recv, slot_home(i), home_chan

    def dkv_plan(i):
        p2 = (p + i) % 32
        return dkvs.at[p2], dkvb.at[r0 * 8 + hl0], dkv_send.at[i], dkv_recv, p2, home_chan

    def st_plan(i):
        g = (head0 + i) % 32
        return (
            stat_in.at[head0], stat_in.at[head0], st_send.at[i], st_recv,
            chip((g // 8) % 2, (g % 8) * 2 + m0), (g // 16) * 2 + core,
        )

    def g_plan(i):
        return gsrc, gin.at[p], g_send.at[i], g_recv, (p + i) % 32, chan

    def each(plan, count, act, first=0):
        lax.fori_loop(first, count, lambda i, _: (act(*plan(i)), 0)[1], 0)

    du[pl.ds(0, BLOCK), :] = cot_ref[...].astype(F32) * go_ref[...].astype(F32)

    def rim_copy(src, dst, j, p2):
        return pltpu.make_async_remote_copy(
            src_ref=src, dst_ref=dst, send_sem=rim_send.at[j], recv_sem=rim_recv.at[j],
            device_id={"ctx": p2, "chan": chan}, device_id_type=pl.DeviceIdType.MESH,
        )

    du_rim = rim_copy(du.at[pl.ds(0, 8)], du.at[pl.ds(BLOCK, 8)], 0, jnp.maximum(p - 1, 0))
    z_rim = rim_copy(zx.at[pl.ds(BLOCK, 8)], zx.at[pl.ds(0, 8)], 1, jnp.minimum(p + 1, 31))

    @pl.when(p > 0)
    def _():
        du_rim.start()

    for hl in range(8):
        cols = slice(hl * HEAD, (hl + 1) * HEAD)
        kvs[hl, 0] = k_ref[:, cols]
        kvs[hl, 1] = v_ref[:, cols]
        qs[hl] = q_ref[:, cols]
    each(kv_plan, 32, send)
    each(q_plan, 8, send)

    group_of = lax.broadcasted_iota(jnp.int32, (128, 1024), 1) // 8
    spread = (group_of == lax.broadcasted_iota(jnp.int32, (128, 1024), 0)).astype(F32)
    taps = dot(taps_ref[...], spread, 0, 0, lax.Precision.HIGHEST)
    gain = gain_ref[...]

    @pl.when(p == 31)
    def _():
        du[pl.ds(BLOCK, 8), :] = jnp.zeros((8, 1024), F32)

    @pl.when(p < 31)
    def _():
        du_rim.wait_recv()

    for hl in range(8):
        cols = slice(hl * HEAD, (hl + 1) * HEAD)
        total = taps[0:1, cols] * du[pl.ds(0, BLOCK), cols]
        for lag in range(1, FILT):
            total = total + taps[lag : lag + 1, cols] * du[pl.ds(lag, BLOCK), cols]
        dz[:, cols] = total
        ssrc[hl] = (total * gi_ref[:, cols].astype(F32) * gain[:, cols]).astype(BF16)
    each(s_plan, 8, send)

    arrived(kvb, kv_recv)
    arrived(qb, q_recv)
    below = lax.broadcasted_iota(jnp.int32, (CHUNK, CHUNK), 0) <= lax.broadcasted_iota(
        jnp.int32, (CHUNK, CHUNK), 1
    )

    def keys_of(kt):
        return kvb[pl.ds(kt * 4, 4), 0].reshape(CHUNK, HEAD)

    def values_of(kt):
        return kvb[pl.ds(kt * 4, 4), 1].reshape(CHUNK, HEAD)

    s_waited = False
    for qc in range(2):
        chunk = r0 if qc == 0 else 7 - r0
        rows = slice(qc * CHUNK, (qc + 1) * CHUNK)
        q_rows = qb[pl.ds(qc * 4, 4)].reshape(CHUNK, HEAD)

        def forward(kt, carry, masked, q_rows=q_rows):
            top, norm, acc = carry
            s = dot(keys_of(kt), q_rows, 1, 1)
            if masked:
                s = jnp.where(below, s, NEG)
            new_top = jnp.maximum(top, jnp.max(s, axis=0, keepdims=True))
            w = jnp.exp2(s * SCALE2 - new_top * SCALE2)
            fade = jnp.exp2((top - new_top) * SCALE2)
            norm = norm * fade + jnp.sum(w, axis=0, keepdims=True)
            acc = acc * fade + dot(values_of(kt), w.astype(BF16), 0, 0)
            return new_top, norm, acc

        carry = (
            jnp.full((1, CHUNK), NEG, F32), jnp.zeros((1, CHUNK), F32), jnp.zeros((HEAD, CHUNK), F32)
        )
        carry = lax.fori_loop(0, chunk, lambda kt, c: forward(kt, c, False), carry)
        top, norm, acc = forward(chunk, carry, True)
        out = (acc * (1.0 / norm)).astype(BF16)
        out_wide = out.astype(F32)
        ot[:, rows] = out_wide
        lse2[:, rows] = top * SCALE2 + jnp.log2(norm)
        osrc[pl.ds(qc * 4, 4)] = out_wide.T.astype(BF16).reshape(4, HEAD, HEAD)
        if not s_waited:
            arrived(sb, s_recv)
            s_waited = True
        s_t = sb[pl.ds(qc * 4, 4)].reshape(CHUNK, HEAD).astype(F32).T
        squares = jnp.sum(out_wide * out_wide, axis=0, keepdims=True)
        dots = jnp.sum(s_t * out_wide, axis=0, keepdims=True)
        for j in range(4):
            at = slice(j * HEAD, (j + 1) * HEAD)
            stat_in[head0, 0, qc * 4 + j : qc * 4 + j + 1, :] = squares[:, at]
            stat_in[head0, 1, qc * 4 + j : qc * 4 + j + 1, :] = dots[:, at]

    each(st_plan, 32, send, 1)
    each(o_plan, 8, send)
    arrived(stat_in.at[pl.ds(0, 31)], st_recv)
    tot[...] = jnp.sum(stat_in[...], axis=0)

    home_slot = jnp.where(r0 % 2 == hl0 // 4, hl0 % 4, 4 + hl0 % 4)
    h_args = (tot, hst, h_send, h_recv, slot_home(home_slot), home_chan)
    send(*h_args)

    rstd_all = lax.rsqrt(tot[0] / WIDTH + EPS)
    drop_all = rstd_all * rstd_all * rstd_all * tot[1] / WIDTH

    def clear(kt, _):
        dk_acc[pl.ds(kt * CHUNK, CHUNK), :] = jnp.zeros((CHUNK, HEAD), F32)
        dv_acc[pl.ds(kt * CHUNK, CHUNK), :] = jnp.zeros((CHUNK, HEAD), F32)
        return 0

    lax.fori_loop(0, 8, clear, 0)
    for qc in range(2):
        chunk = r0 if qc == 0 else 7 - r0
        rows = slice(qc * CHUNK, (qc + 1) * CHUNK)
        q_rows = qb[pl.ds(qc * 4, 4)].reshape(CHUNK, HEAD)
        s_t = sb[pl.ds(qc * 4, 4)].reshape(CHUNK, HEAD).astype(F32).T
        lanes = lambda a: jnp.concatenate([a[qc * 4 + j : qc * 4 + j + 1] for j in range(4)], axis=1)
        out_wide = ot[:, rows]
        d_out_t = (lanes(rstd_all) * s_t - out_wide * lanes(drop_all)).astype(BF16)
        d_wide = d_out_t.astype(F32)
        delta = jnp.sum(d_wide * out_wide, axis=0, keepdims=True)
        d_rows = d_wide.T.astype(BF16)
        lse_row = lse2[:, rows]

        def backward(kt, dq_t, masked, q_rows=q_rows, d_out_t=d_out_t, d_rows=d_rows, delta=delta,
                     lse_row=lse_row):
            k_rows = keys_of(kt)
            s = dot(k_rows, q_rows, 1, 1)
            if masked:
                s = jnp.where(below, s, NEG)
            w = jnp.exp2(s * SCALE2 - lse_row)
            d_w = dot(values_of(kt), d_out_t, 1, 0)
            d_s = (w * (d_w - delta)).astype(BF16)
            at = pl.ds(pl.multiple_of(kt * CHUNK, CHUNK), CHUNK)
            dk_acc[at, :] += dot(d_s, q_rows, 1, 0)
            dv_acc[at, :] += dot(w.astype(BF16), d_rows, 1, 0)
            return dq_t + dot(k_rows, d_s, 0, 0)

        dq_t = jnp.zeros((HEAD, CHUNK), F32)
        dq_t = lax.fori_loop(0, chunk, lambda kt, c: backward(kt, c, False), dq_t)
        dq_t = backward(chunk, dq_t, True)
        dqs[pl.ds(qc * 4, 4)] = (dq_t * SCALE).T.astype(BF16).reshape(4, HEAD, HEAD)

    def to_low(kt, _):
        at = pl.ds(pl.multiple_of(kt * CHUNK, CHUNK), CHUNK)
        dkvs[pl.ds(kt * 4, 4), 0] = (dk_acc[at, :] * SCALE).astype(BF16).reshape(4, HEAD, HEAD)
        dkvs[pl.ds(kt * 4, 4), 1] = dv_acc[at, :].astype(BF16).reshape(4, HEAD, HEAD)
        return 0

    lax.fori_loop(0, 8, to_low, 0)
    each(dkv_plan, 32, send)
    each(dq_plan, 8, send)

    arrived(ob, o_recv)
    arrived(hst, h_recv)
    square_row = hst[0, pl.ds(own_slot, 1), :]
    rstd_row = lax.rsqrt(square_row / WIDTH + EPS)
    rstd = jnp.broadcast_to(rstd_row, (BLOCK, BLOCK)).T
    for hl in range(8):
        cols = slice(hl * HEAD, (hl + 1) * HEAD)
        a_hat = ob[hl].astype(F32) * rstd
        normed = a_hat * gain[:, cols]
        gate = gi_ref[:, cols].astype(F32)
        zx[pl.ds(8, BLOCK), cols] = gate * normed
        ggi_ref[:, cols] = (dz[:, cols] * normed).astype(BF16)
        gsrc[1, hl : hl + 1, :] = jnp.sum(dz[:, cols] * gate * a_hat, axis=0, keepdims=True)

    @pl.when(p < 31)
    def _():
        z_rim.start()

    @pl.when(p == 0)
    def _():
        zx[pl.ds(0, 8), :] = jnp.zeros((8, 1024), F32)

    @pl.when(p > 0)
    def _():
        z_rim.wait_recv()

    tap_sums = []
    for hl in range(8):
        cols = slice(hl * HEAD, (hl + 1) * HEAD)
        d_conv = du[pl.ds(0, BLOCK), cols]
        conv = jnp.zeros((BLOCK, HEAD), F32)
        sums = []
        for lag in range(FILT):
            shifted = zx[pl.ds(8 - lag, BLOCK), cols]
            conv = conv + taps[lag : lag + 1, cols] * shifted
            sums.append(jnp.sum(d_conv * shifted, axis=0, keepdims=True))
        sums.append(jnp.zeros((1, HEAD), F32))
        tap_sums.append(jnp.concatenate(sums, axis=0))
        mixed_ref[:, cols] = (go_ref[:, cols].astype(F32) * conv).astype(BF16)
        ggo_ref[:, cols] = (cot_ref[:, cols].astype(F32) * conv).astype(BF16)
    gsrc[0] = dot(jnp.concatenate(tap_sums, axis=1), spread, 1, 1, lax.Precision.HIGHEST)
    each(g_plan, 32, send, 1)

    arrived(gin.at[pl.ds(0, 31)], g_recv)
    gin[p] = gsrc[...]
    g_total = jnp.sum(gin[...], axis=0)
    gf_ref[...] = g_total[0]
    gg_ref[...] = g_total[1]
    arrived(dqb, dq_recv)
    arrived(dkvb, dkv_recv)
    for hl in range(8):
        cols = slice(hl * HEAD, (hl + 1) * HEAD)
        gq_ref[:, cols] = dqb[hl]
        for which, out_ref in ((0, gk_ref), (1, gv_ref)):
            total = dkvb[hl, which].astype(F32)
            for r in range(1, 4):
                total = total + dkvb[r * 8 + hl, which].astype(F32)
            out_ref[:, cols] = total.astype(BF16)

    each(kv_plan, 32, sent)
    each(q_plan, 8, sent)
    each(s_plan, 8, sent)
    each(st_plan, 32, sent, 1)
    each(o_plan, 8, sent)
    sent(*h_args)
    each(dkv_plan, 32, sent)
    each(dq_plan, 8, sent)
    each(g_plan, 32, sent, 1)

    @pl.when(p > 0)
    def _():
        du_rim.wait_send()

    @pl.when(p < 31)
    def _():
        z_rim.wait_send()


def shards(queries, key_rows, value_rows, gate_in, gate_out, kernel_taps, norm_gain, cotangent):
    rows = jax.ShapeDtypeStruct((BLOCK, 1024), BF16)
    vmem = pl.BlockSpec(memory_space=pltpu.VMEM)
    tile = (HEAD, HEAD)
    dma = pltpu.SemaphoreType.DMA
    outs = pl.pallas_call(
        kernel,
        out_shape=[rows] * 6 + [jax.ShapeDtypeStruct((8, 128), F32)] * 2,
        in_specs=[vmem] * 8,
        out_specs=[vmem] * 8,
        scratch_shapes=[
            pltpu.VMEM((8, 2, *tile), BF16),
            pltpu.VMEM((8, *tile), BF16),
            pltpu.VMEM((8, *tile), BF16),
            pltpu.VMEM((32, 2, *tile), BF16),
            pltpu.VMEM((8, *tile), BF16),
            pltpu.VMEM((8, *tile), BF16),
            pltpu.VMEM((BLOCK + 8, 1024), F32),
            pltpu.VMEM((BLOCK, 1024), F32),
            pltpu.VMEM((HEAD, 1024), F32),
            pltpu.VMEM((1, 1024), F32),
            pltpu.VMEM((8, *tile), BF16),
            pltpu.VMEM((8, *tile), BF16),
            pltpu.VMEM((32, 2, 8, 128), F32),
            pltpu.VMEM((2, 8, 128), F32),
            pltpu.VMEM((2, 8, 128), F32),
            pltpu.VMEM((8, *tile), BF16),
            pltpu.VMEM((8, *tile), BF16),
            pltpu.VMEM((4096, HEAD), F32),
            pltpu.VMEM((4096, HEAD), F32),
            pltpu.VMEM((32, 2, *tile), BF16),
            pltpu.VMEM((32, 2, *tile), BF16),
            pltpu.VMEM((BLOCK + 8, 1024), F32),
            pltpu.VMEM((2, 8, 128), F32),
            pltpu.VMEM((32, 2, 8, 128), F32),
            dma((32,)), dma((8,)), dma((8,)), dma((8,)), dma((32,)), dma, dma((8,)), dma((32,)), dma((32,)),
            dma((2,)),
            dma, dma, dma, dma, dma, dma, dma, dma, dma, dma((2,)),
        ],
        compiler_params=pltpu.CompilerParams(has_side_effects=True, vmem_limit_bytes=56 * 1024 * 1024),
        name="hyena",
    )(
        queries, key_rows, value_rows, gate_in, gate_out, kernel_taps, norm_gain.reshape(1, -1), cotangent
    )
    mixed, gq, gk, gv, ggi, ggo, gf, gg = outs
    return mixed, gq, gk, gv, ggi, ggo, gf[:FILT].T, gg.reshape(-1)


def solution(mesh):
    wide = P("ctx", "chan")
    thin = (P("chan", None), P("chan"))
    return jax.shard_map(
        shards, mesh=mesh, in_specs=(wide,) * 5 + thin + (wide,), out_specs=(wide,) * 6 + thin, check_vma=False
    )
```

```python
import functools
import math

import jax
import jax.numpy as jnp
from jax import lax
from jax.experimental import pallas as pl
from jax.experimental.pallas import tpu as pltpu
from jax.sharding import PartitionSpec as P

HEAD = 128
FILT = 7
WIDTH = 4096
EPS = 1e-06
NEG = -1e30
SCALE = HEAD ** (-0.5)
SCALE2 = SCALE * math.log2(math.e)
BLOCK = 128
CHUNK = 512
F32 = jnp.float32
BF16 = jnp.bfloat16


def dot(a, b, ca, cb, precision=None):
    return lax.dot_general(
        a, b, (((ca,), (cb,)), ((), ())), preferred_element_type=F32, precision=precision
    )


def kernel(
    q_any, k_any, v_any, gi_any, go_any, taps_ref, gain_ref, cot_any,
    mixed_ref, gq_ref, gk_ref, gv_ref, ggi_ref, ggo_ref, gf_ref, gg_ref,
    kvs, qs, ssrc, kvb, qb, sb, du, dz, ot, lse2, osrc, ob, stat_in, tot, hst,
    dqs, dqb, dq_acc, d_out_t, d_rows, delta, kv_acc, sibs, sibb, dkvs, dkvb, zx, gsrc, gin,
    gi_ref, go_ref, cot_ref, wbuf, tops, in_sem, relay_send, relay_recv, sib_send, sib_recv,
    kv_send, q_send, s_send, o_send, st_send, h_send, dq_send, dkv_send, g_send, rim_send,
    kv_recv, q_recv, s_recv, o_recv, st_recv, h_recv, dq_recv, dkv_recv, g_recv, rim_recv,
):
    p = lax.axis_index("ctx")
    chan = lax.axis_index("chan")
    zh, core = chan // 2, chan % 2
    x, z, y = p // 8, (p // 4) % 2, p % 4
    host = x * 4 + y
    hl0, m0 = host // 2, host % 2
    home_chan = zh * 2 + z
    r0 = m0 * 2 + core
    head0 = home_chan * 8 + hl0

    def chip(bit, e):
        return (e // 4) * 8 + bit * 4 + e % 4

    def send(src, dst, send_sem, recv_sem, p2, chan2):
        own = jnp.logical_and(p2 == p, chan2 == chan)

        @pl.when(own)
        def _():
            pltpu.make_async_copy(src, dst, recv_sem).start()

        @pl.when(jnp.logical_not(own))
        def _():
            pltpu.make_async_remote_copy(
                src_ref=src, dst_ref=dst, send_sem=send_sem, recv_sem=recv_sem,
                device_id={"ctx": p2, "chan": chan2}, device_id_type=pl.DeviceIdType.MESH,
            ).start()

    def sent(src, dst, send_sem, recv_sem, p2, chan2):
        own = jnp.logical_and(p2 == p, chan2 == chan)

        @pl.when(jnp.logical_not(own))
        def _():
            pltpu.make_async_remote_copy(
                src_ref=src, dst_ref=dst, send_sem=send_sem, recv_sem=recv_sem,
                device_id={"ctx": p2, "chan": chan2}, device_id_type=pl.DeviceIdType.MESH,
            ).wait_send()

    def arrived(buf, recv_sem):
        pltpu.make_async_copy(buf, buf, recv_sem).wait()

    def kv_plan(i):
        e = (host + i) % 16
        return (
            kvs.at[e // 2], kvb.at[p], kv_send.at[i], kv_recv.at[p // 2],
            chip(core, e), zh * 2 + p % 2,
        )

    def relay_plan(i):
        e = (host - 2 * (i // 2) - (host + core) % 2 + 16) % 16
        source = chip(i % 2, e)
        return (
            kvb.at[source], kvb.at[source], relay_send.at[i], relay_recv,
            p, zh * 2 + 1 - core, kv_recv.at[source // 2],
        )

    def relay(block, dst, send_sem, recv_sem, p2, chan2, landed):
        arrived(block, landed)
        send(block, dst, send_sem, recv_sem, p2, chan2)

    own_chunk = p // 4
    own_r = jnp.minimum(own_chunk, 7 - own_chunk)
    own_slot = (own_chunk // 4) * 4 + p % 4

    def q_plan(i):
        hl = (hl0 + i) % 8
        return (
            qs.at[hl], qb.at[own_slot], q_send.at[i], q_recv,
            chip(core, hl * 2 + own_r // 2), zh * 2 + own_r % 2,
        )

    def s_plan(i):
        hl = (hl0 + i) % 8
        return (
            ssrc.at[hl], sb.at[own_slot], s_send.at[i], s_recv,
            chip(core, hl * 2 + own_r // 2), zh * 2 + own_r % 2,
        )

    def slot_home(slot):
        return jnp.where(slot < 4, r0 * 4 + slot, (7 - r0) * 4 + slot - 4)

    def o_plan(i):
        return osrc.at[i], ob.at[hl0], o_send.at[i], o_recv, slot_home(i), home_chan

    def dq_plan(i):
        return dqs.at[i], dqb.at[hl0], dq_send.at[i], dq_recv, slot_home(i), home_chan

    last_chunk = 7 - 2 * m0

    def dkv_plan(i):
        return (
            dkvs.at[i // 4, i % 4], dkvb.at[m0 * 8 + hl0], dkv_send.at[i], dkv_recv,
            ((i // 4) * 2 + core) * 4 + i % 4, home_chan,
        )

    def sib_copy(i):
        return pltpu.make_async_remote_copy(
            src_ref=sibs.at[i], dst_ref=sibb.at[i], send_sem=sib_send.at[i], recv_sem=sib_recv.at[i],
            device_id={"ctx": p, "chan": zh * 2 + 1 - core}, device_id_type=pl.DeviceIdType.MESH,
        )

    def sib_sent(i):
        @pl.when(i * 2 + 1 - core <= 7 - r0)
        def _():
            sib_copy(i).wait_send()

    def dkv_sent(i):
        @pl.when((i // 4) * 2 + core <= last_chunk)
        def _():
            sent(*dkv_plan(i))

    def st_plan(i):
        g = (head0 + i) % 32
        return (
            stat_in.at[head0], stat_in.at[head0], st_send.at[i], st_recv,
            chip((g // 8) % 2, (g % 8) * 2 + m0), (g // 16) * 2 + core,
        )

    def g_plan(i):
        return gsrc, gin.at[p], g_send.at[i], g_recv, (p + i) % 32, chan

    def each(plan, count, act, first=0):
        lax.fori_loop(first, count, lambda i, _: (act(*plan(i)), 0)[1], 0)

    barrier = pltpu.get_barrier_semaphore()

    def greet(i, _):
        pl.semaphore_signal(
            barrier, inc=1, device_id={"ctx": (p + i // 2) % 32, "chan": zh * 2 + (core + i) % 2},
            device_id_type=pl.DeviceIdType.MESH,
        )
        return 0

    def greet_far(i, _):
        pl.semaphore_signal(
            barrier, inc=1, device_id={"ctx": i * 2 + m0, "chan": (1 - zh) * 2 + core},
            device_id_type=pl.DeviceIdType.MESH,
        )
        return 0

    lax.fori_loop(1, 64, greet, 0)
    lax.fori_loop(0, 16, greet_far, 0)
    wide_in = [
        pltpu.make_async_copy(src, dst, in_sem.at[j])
        for j, (src, dst) in enumerate(((cot_any, cot_ref), (go_any, go_ref), (gi_any, gi_ref)))
    ]
    for copy in wide_in:
        copy.start()
    for hl in range(8):
        cols = slice(hl * HEAD, (hl + 1) * HEAD)
        pltpu.make_async_copy(k_any.at[:, cols], kvs.at[hl, 0], in_sem.at[3]).start()
        pltpu.make_async_copy(v_any.at[:, cols], kvs.at[hl, 1], in_sem.at[3]).start()
        pltpu.make_async_copy(q_any.at[:, cols], qs.at[hl], in_sem.at[4]).start()
    wide_in[0].wait()
    wide_in[1].wait()
    du[pl.ds(0, BLOCK), :] = cot_ref[...].astype(F32) * go_ref[...].astype(F32)

    def rim_copy(src, dst, j, p2):
        return pltpu.make_async_remote_copy(
            src_ref=src, dst_ref=dst, send_sem=rim_send.at[j], recv_sem=rim_recv.at[j],
            device_id={"ctx": p2, "chan": chan}, device_id_type=pl.DeviceIdType.MESH,
        )

    du_rim = rim_copy(du.at[pl.ds(0, 8)], du.at[pl.ds(BLOCK, 8)], 0, jnp.maximum(p - 1, 0))
    z_rim = rim_copy(zx.at[pl.ds(BLOCK, 8)], zx.at[pl.ds(0, 8)], 1, jnp.minimum(p + 1, 31))

    group_of = lax.broadcasted_iota(jnp.int32, (128, 1024), 1) // 8
    spread = (group_of == lax.broadcasted_iota(jnp.int32, (128, 1024), 0)).astype(F32)
    taps = dot(taps_ref[...], spread, 1, 0, lax.Precision.HIGHEST)
    gain = gain_ref[...]

    pltpu.make_async_copy(kvs, kvs, in_sem.at[3]).wait()
    pltpu.make_async_copy(qs, qs, in_sem.at[4]).wait()
    wide_in[2].wait()
    pl.semaphore_wait(barrier, 79)

    @pl.when(p > 0)
    def _():
        du_rim.start()

    each(kv_plan, 16, send)
    each(q_plan, 8, send)

    @pl.when(p == 31)
    def _():
        du[pl.ds(BLOCK, 8), :] = jnp.zeros((8, 1024), F32)

    @pl.when(p < 31)
    def _():
        du_rim.wait_recv()

    for hl in range(8):
        cols = slice(hl * HEAD, (hl + 1) * HEAD)
        total = taps[0:1, cols] * du[pl.ds(0, BLOCK), cols]
        for lag in range(1, FILT):
            total = total + taps[lag : lag + 1, cols] * du[pl.ds(lag, BLOCK), cols]
        dz[:, cols] = total
        ssrc[hl] = (total * gi_ref[:, cols].astype(F32) * gain[:, cols]).astype(BF16)

    each(relay_plan, 16, relay)
    each(s_plan, 8, send)
    arrived(kvb.at[pl.ds(0, 16)], relay_recv)
    arrived(qb, q_recv)
    below = lax.broadcasted_iota(jnp.int32, (CHUNK, CHUNK), 0) <= lax.broadcasted_iota(
        jnp.int32, (CHUNK, CHUNK), 1
    )

    def keys_of(kt):
        return kvb[pl.ds(kt * 4, 4), 0].reshape(CHUNK, HEAD)

    def values_of(kt):
        return kvb[pl.ds(kt * 4, 4), 1].reshape(CHUNK, HEAD)

    s_waited = False
    for qc in range(2):
        chunk = r0 if qc == 0 else 7 - r0
        rows = slice(qc * CHUNK, (qc + 1) * CHUNK)
        q_rows = qb[pl.ds(qc * 4, 4)].reshape(CHUNK, HEAD)

        def forward(kt, carry, masked, q_rows=q_rows, qc=qc):
            top, norm, acc = carry
            s = dot(keys_of(kt), q_rows, 1, 1)
            if masked:
                s = jnp.where(below, s, NEG)
            new_top = jnp.maximum(top, jnp.max(s, axis=0, keepdims=True))
            w = jnp.exp2(s * SCALE2 - new_top * SCALE2)
            w_low = w.astype(BF16)
            wbuf[qc * 8 + kt] = w_low
            tops[qc * 8 + kt] = new_top
            fade = jnp.exp2((top - new_top) * SCALE2)
            norm = norm * fade + jnp.sum(w, axis=0, keepdims=True)
            acc = acc * fade + dot(values_of(kt), w_low, 0, 0)
            return new_top, norm, acc

        carry = (
            jnp.full((1, CHUNK), NEG, F32), jnp.zeros((1, CHUNK), F32), jnp.zeros((HEAD, CHUNK), F32)
        )
        carry = lax.fori_loop(0, chunk, lambda kt, c: forward(kt, c, False), carry)
        top, norm, acc = forward(chunk, carry, True)
        out = (acc * (1.0 / norm)).astype(BF16)
        out_wide = out.astype(F32)
        ot[:, rows] = out_wide
        lse2[:, rows] = top * SCALE2 + jnp.log2(norm)
        osrc[pl.ds(qc * 4, 4)] = out_wide.T.astype(BF16).reshape(4, HEAD, HEAD)
        if not s_waited:
            arrived(sb, s_recv)
            s_waited = True
        s_t = sb[pl.ds(qc * 4, 4)].reshape(CHUNK, HEAD).astype(F32).T
        squares = jnp.sum(out_wide * out_wide, axis=0, keepdims=True)
        dots = jnp.sum(s_t * out_wide, axis=0, keepdims=True)
        for j in range(4):
            at = slice(j * HEAD, (j + 1) * HEAD)
            stat_in[head0, 0, qc * 4 + j : qc * 4 + j + 1, :] = squares[:, at]
            stat_in[head0, 1, qc * 4 + j : qc * 4 + j + 1, :] = dots[:, at]

    each(st_plan, 32, send, 1)
    each(o_plan, 8, send)
    arrived(stat_in.at[pl.ds(0, 31)], st_recv)
    tot[...] = jnp.sum(stat_in[...], axis=0)

    home_slot = jnp.where(r0 % 2 == hl0 // 4, hl0 % 4, 4 + hl0 % 4)
    h_args = (tot, hst, h_send, h_recv, slot_home(home_slot), home_chan)
    send(*h_args)

    rstd_all = lax.rsqrt(tot[0] / WIDTH + EPS)
    drop_all = rstd_all * rstd_all * rstd_all * tot[1] / WIDTH

    for qc in range(2):
        rows = slice(qc * CHUNK, (qc + 1) * CHUNK)
        s_t = sb[pl.ds(qc * 4, 4)].reshape(CHUNK, HEAD).astype(F32).T
        out_wide = ot[:, rows]

        def lanes(a, qc=qc):
            return jnp.concatenate([a[qc * 4 + j : qc * 4 + j + 1] for j in range(4)], axis=1)

        d_low = (lanes(rstd_all) * s_t - out_wide * lanes(drop_all)).astype(BF16)
        d_wide = d_low.astype(F32)
        delta[:, rows] = jnp.sum(d_wide * out_wide, axis=0, keepdims=True)
        d_out_t[:, rows] = d_low
        d_rows[rows, :] = d_wide.T.astype(BF16)
        dq_acc[:, rows] = jnp.zeros((HEAD, CHUNK), F32)

    def backward(qc, kt, slot):
        rows = slice(qc * CHUNK, (qc + 1) * CHUNK)
        q_rows = qb[pl.ds(qc * 4, 4)].reshape(CHUNK, HEAD)
        k_rows = keys_of(kt)
        w = wbuf[qc * 8 + kt].astype(F32) * jnp.exp2(tops[qc * 8 + kt] * SCALE2 - lse2[:, rows])
        d_w = dot(values_of(kt), d_out_t[:, rows], 1, 0)
        d_s = (w * (d_w - delta[:, rows])).astype(BF16)
        d_k = dot(d_s, q_rows, 1, 0)
        d_v = dot(w.astype(BF16), d_rows[rows, :], 1, 0)
        dq_acc[:, rows] += dot(k_rows, d_s, 0, 0)
        if qc == 1:
            kv_acc[slot, 0] = d_k
            kv_acc[slot, 1] = d_v
        else:
            kv_acc[slot, 0] += d_k
            kv_acc[slot, 1] += d_v

    def finish(kt, slot):
        @pl.when(jnp.logical_and(kt % 2 == core, kt <= last_chunk))
        def _():
            sib_copy(kt // 2).wait_recv()
            for which, scale in ((0, SCALE), (1, 1.0)):
                both = kv_acc[slot, which] * scale + sibb[kt // 2, which].astype(F32)
                dkvs[kt // 2, :, which] = both.astype(BF16).reshape(4, HEAD, HEAD)
            for j in range(4):
                send(*dkv_plan((kt // 2) * 4 + j))

    def key_chunk(t, _):
        kt, slot = (hl0 + t) % 8, t % 2
        for qc in (1, 0):
            chunk = r0 if qc == 0 else 7 - r0

            @pl.when(kt <= chunk)
            def _():
                backward(qc, kt, slot)

        @pl.when(jnp.logical_and(kt % 2 != core, kt <= 7 - r0))
        def _():
            for which, scale in ((0, SCALE), (1, 1.0)):
                sibs[kt // 2, which] = (kv_acc[slot, which] * scale).astype(BF16)
            sib_copy(kt // 2).start()

        @pl.when(jnp.logical_and(kt % 2 == core, kt > 7 - r0))
        def _():
            kv_acc[slot] = jnp.zeros((2, CHUNK, HEAD), F32)

        @pl.when(t > 0)
        def _():
            finish((kt + 7) % 8, 1 - slot)

        return 0

    lax.fori_loop(0, 8, key_chunk, 0)
    finish((hl0 + 7) % 8, 1)
    for qc in range(2):
        dq = dq_acc[:, qc * CHUNK : (qc + 1) * CHUNK] * SCALE
        dqs[pl.ds(qc * 4, 4)] = dq.T.astype(BF16).reshape(4, HEAD, HEAD)
    each(dq_plan, 8, send)

    arrived(ob, o_recv)
    arrived(hst, h_recv)
    square_row = hst[0, pl.ds(own_slot, 1), :]
    rstd_row = lax.rsqrt(square_row / WIDTH + EPS)
    rstd = jnp.broadcast_to(rstd_row, (BLOCK, BLOCK)).T
    for hl in range(8):
        cols = slice(hl * HEAD, (hl + 1) * HEAD)
        a_hat = ob[hl].astype(F32) * rstd
        normed = a_hat * gain[:, cols]
        gate = gi_ref[:, cols].astype(F32)
        zx[pl.ds(8, BLOCK), cols] = gate * normed
        ggi_ref[:, cols] = (dz[:, cols] * normed).astype(BF16)
        gsrc[1, hl : hl + 1, :] = jnp.sum(dz[:, cols] * gate * a_hat, axis=0, keepdims=True)

    @pl.when(p < 31)
    def _():
        z_rim.start()

    @pl.when(p == 0)
    def _():
        zx[pl.ds(0, 8), :] = jnp.zeros((8, 1024), F32)

    @pl.when(p > 0)
    def _():
        z_rim.wait_recv()

    tap_sums = []
    for hl in range(8):
        cols = slice(hl * HEAD, (hl + 1) * HEAD)
        d_conv = du[pl.ds(0, BLOCK), cols]
        conv = jnp.zeros((BLOCK, HEAD), F32)
        sums = []
        for lag in range(FILT):
            shifted = zx[pl.ds(8 - lag, BLOCK), cols]
            conv = conv + taps[lag : lag + 1, cols] * shifted
            sums.append(jnp.sum(d_conv * shifted, axis=0, keepdims=True))
        sums.append(jnp.zeros((1, HEAD), F32))
        tap_sums.append(jnp.concatenate(sums, axis=0))
        mixed_ref[:, cols] = (go_ref[:, cols].astype(F32) * conv).astype(BF16)
        ggo_ref[:, cols] = (cot_ref[:, cols].astype(F32) * conv).astype(BF16)
    gsrc[0] = dot(jnp.concatenate(tap_sums, axis=1), spread, 1, 1, lax.Precision.HIGHEST)
    each(g_plan, 32, send, 1)

    arrived(gin.at[pl.ds(0, 31)], g_recv)
    gin[p] = gsrc[...]
    g_total = jnp.sum(gin[...], axis=0)
    gf_ref[...] = g_total[0, :FILT]
    gg_ref[...] = g_total[1]
    arrived(dqb, dq_recv)

    def all_keys(parts):
        arrived(dkvb.at[pl.ds(0, parts * 8)], dkv_recv)
        for hl in range(8):
            cols = slice(hl * HEAD, (hl + 1) * HEAD)
            for which, out_ref in ((0, gk_ref), (1, gv_ref)):
                total = dkvb[hl, which]
                if parts == 2:
                    total = (total.astype(F32) + dkvb[8 + hl, which].astype(F32)).astype(BF16)
                out_ref[:, cols] = total

    for hl in range(8):
        gq_ref[:, hl * HEAD : (hl + 1) * HEAD] = dqb[hl]

    @pl.when(own_chunk <= 5)
    def _():
        all_keys(2)

    @pl.when(own_chunk > 5)
    def _():
        all_keys(1)

    each(kv_plan, 16, sent)
    each(relay_plan, 16, lambda *a: sent(*a[:6]))
    lax.fori_loop(0, 4, lambda i, _: (sib_sent(i), 0)[1], 0)
    each(q_plan, 8, sent)
    each(s_plan, 8, sent)
    each(st_plan, 32, sent, 1)
    each(o_plan, 8, sent)
    sent(*h_args)
    lax.fori_loop(0, 16, lambda i, _: (dkv_sent(i), 0)[1], 0)
    each(dq_plan, 8, sent)
    each(g_plan, 32, sent, 1)

    @pl.when(p > 0)
    def _():
        du_rim.wait_send()

    @pl.when(p < 31)
    def _():
        z_rim.wait_send()


def handed_on(*refs):
    sems = refs[16]
    copies = [pltpu.make_async_copy(refs[i], refs[8 + i], sems.at[i]) for i in range(8)]
    for copy in copies:
        copy.start()
    for copy in copies:
        copy.wait()


def shards(queries, key_rows, value_rows, gate_in, gate_out, kernel_taps, norm_gain, cotangent):
    rows = jax.ShapeDtypeStruct((BLOCK, 1024), BF16)
    vmem = pl.BlockSpec(memory_space=pltpu.VMEM)
    hbm = pl.BlockSpec(memory_space=pl.ANY)
    tile = (HEAD, HEAD)
    dma = pltpu.SemaphoreType.DMA
    outs = pl.pallas_call(
        kernel,
        out_shape=[rows] * 6 + [jax.ShapeDtypeStruct((FILT, 128), F32), jax.ShapeDtypeStruct((8, 128), F32)],
        in_specs=[hbm] * 5 + [vmem] * 2 + [hbm],
        out_specs=[vmem] * 8,
        scratch_shapes=[
            pltpu.VMEM((8, 2, *tile), BF16),
            pltpu.VMEM((8, *tile), BF16),
            pltpu.VMEM((8, *tile), BF16),
            pltpu.VMEM((32, 2, *tile), BF16),
            pltpu.VMEM((8, *tile), BF16),
            pltpu.VMEM((8, *tile), BF16),
            pltpu.VMEM((BLOCK + 8, 1024), F32),
            pltpu.VMEM((BLOCK, 1024), F32),
            pltpu.VMEM((HEAD, 1024), F32),
            pltpu.VMEM((1, 1024), F32),
            pltpu.VMEM((8, *tile), BF16),
            pltpu.VMEM((8, *tile), BF16),
            pltpu.VMEM((32, 2, 8, 128), F32),
            pltpu.VMEM((2, 8, 128), F32),
            pltpu.VMEM((2, 8, 128), F32),
            pltpu.VMEM((8, *tile), BF16),
            pltpu.VMEM((8, *tile), BF16),
            pltpu.VMEM((HEAD, 1024), F32),
            pltpu.VMEM((HEAD, 1024), BF16),
            pltpu.VMEM((1024, HEAD), BF16),
            pltpu.VMEM((1, 1024), F32),
            pltpu.VMEM((2, 2, CHUNK, HEAD), F32),
            pltpu.VMEM((4, 2, CHUNK, HEAD), BF16),
            pltpu.VMEM((4, 2, CHUNK, HEAD), BF16),
            pltpu.VMEM((4, 4, 2, *tile), BF16),
            pltpu.VMEM((16, 2, *tile), BF16),
            pltpu.VMEM((BLOCK + 8, 1024), F32),
            pltpu.VMEM((2, 8, 128), F32),
            pltpu.VMEM((32, 2, 8, 128), F32),
            pltpu.VMEM((BLOCK, 1024), BF16),
            pltpu.VMEM((BLOCK, 1024), BF16),
            pltpu.VMEM((BLOCK, 1024), BF16),
            pltpu.VMEM((16, CHUNK, CHUNK), BF16),
            pltpu.VMEM((16, 1, CHUNK), F32),
            dma((5,)),
            dma((16,)), dma, dma((4,)), dma((4,)),
            dma((16,)), dma((8,)), dma((8,)), dma((8,)), dma((32,)), dma, dma((8,)), dma((16,)), dma((32,)),
            dma((2,)),
            dma((16,)), dma, dma, dma, dma, dma, dma, dma, dma, dma((2,)),
        ],
        compiler_params=pltpu.CompilerParams(collective_id=0, has_side_effects=True, vmem_limit_bytes=56 * 1024 * 1024),
        name="hyena",
    )(
        queries, key_rows, value_rows, gate_in, gate_out, kernel_taps.T, norm_gain.reshape(1, -1), cotangent
    )
    mixed, gq, gk, gv, ggi, ggo, gf, gg = pl.pallas_call(
        handed_on,
        out_shape=[jax.ShapeDtypeStruct(o.shape, o.dtype) for o in outs],
        in_specs=[vmem] * 8,
        out_specs=[pl.BlockSpec(memory_space=pl.ANY)] * 8,
        scratch_shapes=[dma((8,))],
        name="results",
    )(*outs)
    return mixed, gq, gk, gv, ggi, ggo, gf.T, gg.reshape(-1)


def solution(mesh):
    wide = P("ctx", "chan")
    thin = (P("chan", None), P("chan"))
    return jax.shard_map(
        shards, mesh=mesh, in_specs=(wide,) * 5 + thin + (wide,), out_specs=(wide,) * 6 + thin, check_vma=False
    )
```

```python
import functools
import math

import jax
import jax.numpy as jnp
from jax import lax
from jax.experimental import pallas as pl
from jax.experimental.pallas import tpu as pltpu
from jax.sharding import PartitionSpec as P

HEAD = 128
FILT = 7
WIDTH = 4096
EPS = 1e-06
NEG = -1e30
SCALE = HEAD ** (-0.5)
SCALE2 = SCALE * math.log2(math.e)
BLOCK = 128
CHUNK = 512
F32 = jnp.float32
BF16 = jnp.bfloat16


def dot(a, b, ca, cb, precision=None):
    return lax.dot_general(
        a, b, (((ca,), (cb,)), ((), ())), preferred_element_type=F32, precision=precision
    )


def kernel(
    q_any, k_any, v_any, gi_any, go_any, taps_ref, gain_ref, cot_any,
    mixed_ref, gq_ref, gk_ref, gv_ref, ggi_ref, ggo_ref, gf_ref, gg_ref,
    kvs, qs, ssrc, kvb, qb, sb, du, dz, ot, lse2, osrc, ob, sum_sets, sum_heads, tot, hst,
    dqs, dqb, f_top, f_norm, dq_acc, d_out_t, d_rows, delta, kv_acc, sibs, sibb, dkvs, dkvb, zx, g_near, g_far,
    gi_ref, go_ref, cot_ref, wbuf, tops, su_send, su_recv, gx_send, gx_recv, in_sem, relay_send, relay_recv, sib_send, sib_recv,
    kv_send, q_send, s_send, o_send, st_send, h_send, dq_send, dkv_send, g_send, rim_send,
    kv_recv, q_recv, s_recv, o_recv, st_recv, h_recv, dq_recv, dkv_recv, g_recv, rim_recv,
):
    p = lax.axis_index("ctx")
    chan = lax.axis_index("chan")
    zh, core = chan // 2, chan % 2
    x, z, y = p // 8, (p // 4) % 2, p % 4
    host = x * 4 + y
    hl0, m0 = host // 2, host % 2
    home_chan = zh * 2 + z
    r0 = m0 * 2 + core

    def chip(bit, e):
        return (e // 4) * 8 + bit * 4 + e % 4

    def send(src, dst, send_sem, recv_sem, p2, chan2):
        own = jnp.logical_and(p2 == p, chan2 == chan)

        @pl.when(own)
        def _():
            pltpu.make_async_copy(src, dst, recv_sem).start()

        @pl.when(jnp.logical_not(own))
        def _():
            pltpu.make_async_remote_copy(
                src_ref=src, dst_ref=dst, send_sem=send_sem, recv_sem=recv_sem,
                device_id={"ctx": p2, "chan": chan2}, device_id_type=pl.DeviceIdType.MESH,
            ).start()

    def sent(src, dst, send_sem, recv_sem, p2, chan2):
        own = jnp.logical_and(p2 == p, chan2 == chan)

        @pl.when(jnp.logical_not(own))
        def _():
            pltpu.make_async_remote_copy(
                src_ref=src, dst_ref=dst, send_sem=send_sem, recv_sem=recv_sem,
                device_id={"ctx": p2, "chan": chan2}, device_id_type=pl.DeviceIdType.MESH,
            ).wait_send()

    def arrived(buf, recv_sem):
        pltpu.make_async_copy(buf, buf, recv_sem).wait()

    def moved(i, sign):
        step = (i * 5) % 16
        return ((x + sign * (step // 4) + 4) % 4) * 4 + (y + sign * (step % 4) + 4) % 4

    def kv_plan(i):
        e = moved(i, 1)
        return (
            kvs.at[e // 2], kvb.at[p], kv_send.at[i], kv_recv.at[p // 2],
            chip(core, e), zh * 2 + p % 2,
        )

    def relay_source(i):
        return chip(i % 2, moved(i - i % 2 + (y + core) % 2, -1))

    def relay_plan(i):
        source = relay_source(i)
        return (
            kvb.at[source], kvb.at[source], relay_send.at[i], relay_recv,
            p, zh * 2 + 1 - core, kv_recv.at[source // 2],
        )

    last_chunk = 7 - 2 * m0

    def kv_wanted(i, act):
        @pl.when(jnp.logical_or(own_chunk <= 5, (i + y) % 2 == 0))
        def _():
            act(*kv_plan(i))

    def relay_wanted(i, act):
        @pl.when(relay_source(i) // 4 <= last_chunk)
        def _():
            act(*relay_plan(i))

    def loop(count, act, first=0):
        lax.fori_loop(first, count, lambda i, _: (act(i), 0)[1], 0)

    own_chunk = p // 4

    def relay(block, dst, send_sem, recv_sem, p2, chan2, landed):
        arrived(block, landed)
        send(block, dst, send_sem, recv_sem, p2, chan2)

    own_r = jnp.minimum(own_chunk, 7 - own_chunk)
    own_slot = (own_chunk // 4) * 4 + p % 4

    def q_plan(i):
        hl = (hl0 + 3 * i) % 8
        return (
            qs.at[hl], qb.at[own_slot], q_send.at[i], q_recv,
            chip(core, hl * 2 + own_r // 2), zh * 2 + own_r % 2,
        )

    def s_plan(i):
        hl = (hl0 + 3 * i) % 8
        return (
            ssrc.at[hl], sb.at[own_slot], s_send.at[i], s_recv,
            chip(core, hl * 2 + own_r // 2), zh * 2 + own_r % 2,
        )

    def slot_home(slot):
        return jnp.where(slot < 4, r0 * 4 + slot, (7 - r0) * 4 + slot - 4)

    def o_plan(i):
        slot = ((i + x) % 2) * 4 + (y + i // 2) % 4
        return osrc.at[slot], ob.at[hl0], o_send.at[i], o_recv, slot_home(slot), home_chan

    def dq_plan(i):
        slot = ((i + x) % 2) * 4 + (y + i // 2) % 4
        return dqs.at[slot], dqb.at[hl0], dq_send.at[i], dq_recv, slot_home(slot), home_chan

    def dkv_plan(i):
        return (
            dkvs.at[i // 4, i % 4], dkvb.at[m0 * 8 + hl0], dkv_send.at[i], dkv_recv,
            ((i // 4) * 2 + core) * 4 + i % 4, home_chan,
        )

    def sib_copy(i):
        return pltpu.make_async_remote_copy(
            src_ref=sibs.at[i], dst_ref=sibb.at[i], send_sem=sib_send.at[i], recv_sem=sib_recv.at[i],
            device_id={"ctx": p, "chan": zh * 2 + 1 - core}, device_id_type=pl.DeviceIdType.MESH,
        )

    def sib_sent(i):
        @pl.when(i * 2 + 1 - core <= 7 - r0)
        def _():
            sib_copy(i).wait_send()

    def dkv_sent(i):
        @pl.when((i // 4) * 2 + core <= last_chunk)
        def _():
            sent(*dkv_plan(i))

    def st_plan(i):
        g = (home_chan + i) % 4
        return (
            sum_sets.at[home_chan], sum_sets.at[home_chan], st_send.at[i], st_recv,
            chip(g % 2, host), (g // 2) * 2 + core,
        )

    def su_plan(i):
        hl = (hl0 + i) % 8
        return (
            sum_heads.at[hl0], sum_heads.at[hl0], su_send.at[i], su_recv,
            chip(z, hl * 2 + m0), chan,
        )

    def g_plan(i):
        g = (z * 4 + y + i) % 8
        return g_near.at[z * 4 + y], g_near.at[z * 4 + y], g_send.at[i], g_recv, x * 8 + g, chan

    def gx_plan(i):
        return g_far.at[x], g_far.at[x], gx_send.at[i], gx_recv, ((x + i) % 4) * 8 + z * 4 + y, chan

    def each(plan, count, act, first=0):
        lax.fori_loop(first, count, lambda i, _: (act(*plan(i)), 0)[1], 0)

    barrier = pltpu.get_barrier_semaphore()

    def greet(i, _):
        pl.semaphore_signal(
            barrier, inc=1, device_id={"ctx": (p + i // 2) % 32, "chan": zh * 2 + (core + i) % 2},
            device_id_type=pl.DeviceIdType.MESH,
        )
        return 0

    def greet_far(i, _):
        pl.semaphore_signal(
            barrier, inc=1, device_id={"ctx": chip(i, host), "chan": (1 - zh) * 2 + core},
            device_id_type=pl.DeviceIdType.MESH,
        )
        return 0

    lax.fori_loop(1, 64, greet, 0)
    lax.fori_loop(0, 2, greet_far, 0)
    wide_in = [
        pltpu.make_async_copy(src, dst, in_sem.at[j])
        for j, (src, dst) in enumerate(((cot_any, cot_ref), (go_any, go_ref), (gi_any, gi_ref)))
    ]
    for copy in wide_in:
        copy.start()
    for hl in range(8):
        cols = slice(hl * HEAD, (hl + 1) * HEAD)
        pltpu.make_async_copy(k_any.at[:, cols], kvs.at[hl, 0], in_sem.at[3]).start()
        pltpu.make_async_copy(v_any.at[:, cols], kvs.at[hl, 1], in_sem.at[3]).start()
        pltpu.make_async_copy(q_any.at[:, cols], qs.at[hl], in_sem.at[4]).start()
    wide_in[0].wait()
    wide_in[1].wait()
    du[pl.ds(0, BLOCK), :] = cot_ref[...].astype(F32) * go_ref[...].astype(F32)

    def rim_copy(src, dst, j, p2):
        return pltpu.make_async_remote_copy(
            src_ref=src, dst_ref=dst, send_sem=rim_send.at[j], recv_sem=rim_recv.at[j],
            device_id={"ctx": p2, "chan": chan}, device_id_type=pl.DeviceIdType.MESH,
        )

    du_rim = rim_copy(du.at[pl.ds(0, 8)], du.at[pl.ds(BLOCK, 8)], 0, jnp.maximum(p - 1, 0))
    z_rim = rim_copy(zx.at[pl.ds(BLOCK, 8)], zx.at[pl.ds(0, 8)], 1, jnp.minimum(p + 1, 31))

    group_of = lax.broadcasted_iota(jnp.int32, (128, 1024), 1) // 8
    spread = (group_of == lax.broadcasted_iota(jnp.int32, (128, 1024), 0)).astype(F32)
    taps = dot(taps_ref[...], spread, 1, 0, lax.Precision.HIGHEST)
    gain = gain_ref[...]

    pltpu.make_async_copy(kvs, kvs, in_sem.at[3]).wait()
    pltpu.make_async_copy(qs, qs, in_sem.at[4]).wait()
    wide_in[2].wait()
    pl.semaphore_wait(barrier, 65)

    @pl.when(p > 0)
    def _():
        du_rim.start()

    each(q_plan, 8, send)
    loop(16, lambda i: kv_wanted(i, send))

    @pl.when(p == 31)
    def _():
        du[pl.ds(BLOCK, 8), :] = jnp.zeros((8, 1024), F32)

    @pl.when(p < 31)
    def _():
        du_rim.wait_recv()

    for hl in range(8):
        cols = slice(hl * HEAD, (hl + 1) * HEAD)
        total = taps[0:1, cols] * du[pl.ds(0, BLOCK), cols]
        for lag in range(1, FILT):
            total = total + taps[lag : lag + 1, cols] * du[pl.ds(lag, BLOCK), cols]
        dz[:, cols] = total
        ssrc[hl] = (total * gi_ref[:, cols].astype(F32) * gain[:, cols]).astype(BF16)

    below = lax.broadcasted_iota(jnp.int32, (CHUNK, CHUNK), 0) <= lax.broadcasted_iota(
        jnp.int32, (CHUNK, CHUNK), 1
    )

    def keys_of(kt):
        return kvb[pl.ds(kt * 4, 4), 0].reshape(CHUNK, HEAD)

    def values_of(kt):
        return kvb[pl.ds(kt * 4, 4), 1].reshape(CHUNK, HEAD)

    chunks = (r0, 7 - r0)
    f_top[...] = jnp.full((1, 1024), NEG, F32)
    f_norm[...] = jnp.zeros((1, 1024), F32)
    ot[...] = jnp.zeros((HEAD, 1024), F32)

    def forward(qc, kt, masked):
        rows = slice(qc * CHUNK, (qc + 1) * CHUNK)
        s = dot(keys_of(kt), qb[pl.ds(qc * 4, 4)].reshape(CHUNK, HEAD), 1, 1)
        if masked:
            s = jnp.where(below, s, NEG)
        top = f_top[:, rows]
        new_top = jnp.maximum(top, jnp.max(s, axis=0, keepdims=True))
        w = jnp.exp2(s * SCALE2 - new_top * SCALE2)
        w_low = w.astype(BF16)
        wbuf[qc * 8 + kt] = w_low
        tops[qc * 8 + kt] = new_top
        fade = jnp.exp2((top - new_top) * SCALE2)
        f_top[:, rows] = new_top
        f_norm[:, rows] = f_norm[:, rows] * fade + jnp.sum(w, axis=0, keepdims=True)
        ot[:, rows] = ot[:, rows] * fade + dot(values_of(kt), w_low, 0, 0)

    def forward_chunk(kt, _):
        for qc in range(2):

            @pl.when(kt < chunks[qc])
            def _():
                forward(qc, kt, False)

            @pl.when(kt == chunks[qc])
            def _():
                forward(qc, kt, True)

        return 0

    loop(16, lambda i: relay_wanted(i, relay))
    each(s_plan, 8, send)

    @pl.when(m0 == 0)
    def _():
        arrived(kvb.at[pl.ds(0, 16)], relay_recv)

    @pl.when(m0 == 1)
    def _():
        arrived(kvb.at[pl.ds(0, 12)], relay_recv)

    arrived(qb, q_recv)
    lax.fori_loop(0, 8, forward_chunk, 0)
    arrived(sb, s_recv)
    for qc in range(2):
        rows = slice(qc * CHUNK, (qc + 1) * CHUNK)
        norm = f_norm[:, rows]
        out = (ot[:, rows] * (1.0 / norm)).astype(BF16)
        out_wide = out.astype(F32)
        ot[:, rows] = out_wide
        lse2[:, rows] = f_top[:, rows] * SCALE2 + jnp.log2(norm)
        osrc[pl.ds(qc * 4, 4)] = out_wide.T.astype(BF16).reshape(4, HEAD, HEAD)
        s_t = sb[pl.ds(qc * 4, 4)].reshape(CHUNK, HEAD).astype(F32).T
        squares = jnp.sum(out_wide * out_wide, axis=0, keepdims=True)
        dots = jnp.sum(s_t * out_wide, axis=0, keepdims=True)
        for j in range(4):
            at = slice(j * HEAD, (j + 1) * HEAD)
            sum_sets[home_chan, 0, qc * 4 + j : qc * 4 + j + 1, :] = squares[:, at]
            sum_sets[home_chan, 1, qc * 4 + j : qc * 4 + j + 1, :] = dots[:, at]

    each(st_plan, 4, send, 1)
    each(o_plan, 8, send)
    loop(16, lambda i: kv_wanted(i, sent))
    each(q_plan, 8, sent)
    loop(16, lambda i: relay_wanted(i, lambda *a: sent(*a[:6])))
    arrived(sum_sets.at[pl.ds(0, 3)], st_recv)
    sum_heads[hl0] = jnp.sum(sum_sets[...], axis=0)
    each(su_plan, 8, send, 1)
    each(st_plan, 4, sent, 1)
    each(s_plan, 8, sent)
    arrived(sum_heads.at[pl.ds(0, 7)], su_recv)
    tot[...] = jnp.sum(sum_heads[...], axis=0)
    home_slot = jnp.where(r0 % 2 == hl0 // 4, hl0 % 4, 4 + hl0 % 4)
    h_args = (tot, hst, h_send, h_recv, slot_home(home_slot), home_chan)
    send(*h_args)

    rstd_all = lax.rsqrt(tot[0] / WIDTH + EPS)
    drop_all = rstd_all * rstd_all * rstd_all * tot[1] / WIDTH

    for qc in range(2):
        rows = slice(qc * CHUNK, (qc + 1) * CHUNK)
        s_t = sb[pl.ds(qc * 4, 4)].reshape(CHUNK, HEAD).astype(F32).T
        out_wide = ot[:, rows]

        def lanes(a, qc=qc):
            return jnp.concatenate([a[qc * 4 + j : qc * 4 + j + 1] for j in range(4)], axis=1)

        d_low = (lanes(rstd_all) * s_t - out_wide * lanes(drop_all)).astype(BF16)
        d_wide = d_low.astype(F32)
        delta[:, rows] = jnp.sum(d_wide * out_wide, axis=0, keepdims=True)
        d_out_t[:, rows] = d_low
        d_rows[rows, :] = d_wide.T.astype(BF16)
        dq_acc[:, rows] = jnp.zeros((HEAD, CHUNK), F32)

    def backward(qc, kt, slot):
        rows = slice(qc * CHUNK, (qc + 1) * CHUNK)
        q_rows = qb[pl.ds(qc * 4, 4)].reshape(CHUNK, HEAD)
        k_rows = keys_of(kt)
        w = wbuf[qc * 8 + kt].astype(F32) * jnp.exp2(tops[qc * 8 + kt] * SCALE2 - lse2[:, rows])
        d_w = dot(values_of(kt), d_out_t[:, rows], 1, 0)
        d_s = (w * (d_w - delta[:, rows])).astype(BF16)
        d_k = dot(d_s, q_rows, 1, 0)
        d_v = dot(w.astype(BF16), d_rows[rows, :], 1, 0)
        dq_acc[:, rows] += dot(k_rows, d_s, 0, 0)
        if qc == 1:
            kv_acc[slot, 0] = d_k
            kv_acc[slot, 1] = d_v
        else:
            kv_acc[slot, 0] += d_k
            kv_acc[slot, 1] += d_v

    def finish(kt, slot):
        @pl.when(jnp.logical_and(kt % 2 == core, kt <= last_chunk))
        def _():
            sib_copy(kt // 2).wait_recv()
            for which, scale in ((0, SCALE), (1, 1.0)):
                both = kv_acc[slot, which] * scale + sibb[kt // 2, which].astype(F32)
                dkvs[kt // 2, :, which] = both.astype(BF16).reshape(4, HEAD, HEAD)
            loop((kt // 2) * 4 + 4, lambda i: send(*dkv_plan(i)), (kt // 2) * 4)

    first = hl0 + 2 * y

    def key_chunk(t, _):
        kt, slot = (first + t) % 8, t % 2
        for qc in (1, 0):
            @pl.when(kt <= chunks[qc])
            def _():
                backward(qc, kt, slot)

        @pl.when(jnp.logical_and(kt % 2 != core, kt <= 7 - r0))
        def _():
            for which, scale in ((0, SCALE), (1, 1.0)):
                sibs[kt // 2, which] = (kv_acc[slot, which] * scale).astype(BF16)
            sib_copy(kt // 2).start()

        @pl.when(jnp.logical_and(kt % 2 == core, kt > 7 - r0))
        def _():
            kv_acc[slot] = jnp.zeros((2, CHUNK, HEAD), F32)

        @pl.when(t > 0)
        def _():
            finish((kt + 7) % 8, 1 - slot)

        return 0

    lax.fori_loop(0, 4, key_chunk, 0)
    arrived(ob, o_recv)
    arrived(hst, h_recv)
    square_row = hst[0, pl.ds(own_slot, 1), :]
    rstd_row = lax.rsqrt(square_row / WIDTH + EPS)
    rstd = jnp.broadcast_to(rstd_row, (BLOCK, BLOCK)).T
    for hl in range(8):
        cols = slice(hl * HEAD, (hl + 1) * HEAD)
        a_hat = ob[hl].astype(F32) * rstd
        normed = a_hat * gain[:, cols]
        gate = gi_ref[:, cols].astype(F32)
        zx[pl.ds(8, BLOCK), cols] = gate * normed
        ggi_ref[:, cols] = (dz[:, cols] * normed).astype(BF16)
        g_near[z * 4 + y, 1, hl : hl + 1, :] = jnp.sum(dz[:, cols] * gate * a_hat, axis=0, keepdims=True)

    @pl.when(p < 31)
    def _():
        z_rim.start()

    @pl.when(p == 0)
    def _():
        zx[pl.ds(0, 8), :] = jnp.zeros((8, 1024), F32)

    lax.fori_loop(4, 6, key_chunk, 0)
    @pl.when(p > 0)
    def _():
        z_rim.wait_recv()

    tap_sums = []
    for hl in range(8):
        cols = slice(hl * HEAD, (hl + 1) * HEAD)
        d_conv = du[pl.ds(0, BLOCK), cols]
        conv = jnp.zeros((BLOCK, HEAD), F32)
        sums = []
        for lag in range(FILT):
            shifted = zx[pl.ds(8 - lag, BLOCK), cols]
            conv = conv + taps[lag : lag + 1, cols] * shifted
            sums.append(jnp.sum(d_conv * shifted, axis=0, keepdims=True))
        sums.append(jnp.zeros((1, HEAD), F32))
        tap_sums.append(jnp.concatenate(sums, axis=0))
        mixed_ref[:, cols] = (go_ref[:, cols].astype(F32) * conv).astype(BF16)
        ggo_ref[:, cols] = (cot_ref[:, cols].astype(F32) * conv).astype(BF16)
    g_near[z * 4 + y, 0] = dot(jnp.concatenate(tap_sums, axis=1), spread, 1, 1, lax.Precision.HIGHEST)
    each(g_plan, 8, send, 1)
    lax.fori_loop(6, 8, key_chunk, 0)
    finish((first + 7) % 8, 1)
    for qc in range(2):
        dq = dq_acc[:, qc * CHUNK : (qc + 1) * CHUNK] * SCALE
        dqs[pl.ds(qc * 4, 4)] = dq.T.astype(BF16).reshape(4, HEAD, HEAD)
    each(dq_plan, 8, send)
    arrived(g_near.at[pl.ds(0, 7)], g_recv)
    g_far[x] = jnp.sum(g_near[...], axis=0)
    each(gx_plan, 4, send, 1)
    each(o_plan, 8, sent)
    sent(*h_args)
    each(su_plan, 8, sent, 1)
    each(g_plan, 8, sent, 1)
    arrived(g_far.at[pl.ds(0, 3)], gx_recv)
    g_total = jnp.sum(g_far[...], axis=0)
    gf_ref[...] = g_total[0, :FILT]
    gg_ref[...] = g_total[1]
    lax.fori_loop(0, 4, lambda i, _: (sib_sent(i), 0)[1], 0)
    lax.fori_loop(0, 16, lambda i, _: (dkv_sent(i), 0)[1], 0)
    each(dq_plan, 8, sent)
    each(gx_plan, 4, sent, 1)

    @pl.when(p > 0)
    def _():
        du_rim.wait_send()

    @pl.when(p < 31)
    def _():
        z_rim.wait_send()

    arrived(dqb, dq_recv)

    def all_keys(parts):
        arrived(dkvb.at[pl.ds(0, parts * 8)], dkv_recv)
        for hl in range(8):
            cols = slice(hl * HEAD, (hl + 1) * HEAD)
            for which, out_ref in ((0, gk_ref), (1, gv_ref)):
                total = dkvb[hl, which]
                if parts == 2:
                    total = (total.astype(F32) + dkvb[8 + hl, which].astype(F32)).astype(BF16)
                out_ref[:, cols] = total

    for hl in range(8):
        gq_ref[:, hl * HEAD : (hl + 1) * HEAD] = dqb[hl]

    @pl.when(own_chunk <= 5)
    def _():
        all_keys(2)

    @pl.when(own_chunk > 5)
    def _():
        all_keys(1)


def handed_on(*refs):
    held, in_sem, out_sem = refs[16:24], refs[24], refs[25]
    loads = [pltpu.make_async_copy(refs[i], held[i], in_sem.at[i]) for i in range(8)]
    stores = [pltpu.make_async_copy(held[i], refs[8 + i], out_sem.at[i]) for i in range(8)]
    for load in loads:
        load.start()
    for load, store in zip(loads, stores):
        load.wait()
        store.start()
    for store in stores:
        store.wait()


def shards(queries, key_rows, value_rows, gate_in, gate_out, kernel_taps, norm_gain, cotangent):
    rows = jax.ShapeDtypeStruct((BLOCK, 1024), BF16)
    vmem = pl.BlockSpec(memory_space=pltpu.VMEM)
    hbm = pl.BlockSpec(memory_space=pl.ANY)
    tile = (HEAD, HEAD)
    dma = pltpu.SemaphoreType.DMA
    outs = pl.pallas_call(
        kernel,
        out_shape=[rows] * 6 + [jax.ShapeDtypeStruct((FILT, 128), F32), jax.ShapeDtypeStruct((8, 128), F32)],
        in_specs=[hbm] * 5 + [vmem] * 2 + [hbm],
        out_specs=[vmem] * 8,
        scratch_shapes=[
            pltpu.VMEM((8, 2, *tile), BF16),
            pltpu.VMEM((8, *tile), BF16),
            pltpu.VMEM((8, *tile), BF16),
            pltpu.VMEM((32, 2, *tile), BF16),
            pltpu.VMEM((8, *tile), BF16),
            pltpu.VMEM((8, *tile), BF16),
            pltpu.VMEM((BLOCK + 8, 1024), F32),
            pltpu.VMEM((BLOCK, 1024), F32),
            pltpu.VMEM((HEAD, 1024), F32),
            pltpu.VMEM((1, 1024), F32),
            pltpu.VMEM((8, *tile), BF16),
            pltpu.VMEM((8, *tile), BF16),
            pltpu.VMEM((4, 2, 8, 128), F32),
            pltpu.VMEM((8, 2, 8, 128), F32),
            pltpu.VMEM((2, 8, 128), F32),
            pltpu.VMEM((2, 8, 128), F32),
            pltpu.VMEM((8, *tile), BF16),
            pltpu.VMEM((8, *tile), BF16),
            pltpu.VMEM((1, 1024), F32),
            pltpu.VMEM((1, 1024), F32),
            pltpu.VMEM((HEAD, 1024), F32),
            pltpu.VMEM((HEAD, 1024), BF16),
            pltpu.VMEM((1024, HEAD), BF16),
            pltpu.VMEM((1, 1024), F32),
            pltpu.VMEM((2, 2, CHUNK, HEAD), F32),
            pltpu.VMEM((4, 2, CHUNK, HEAD), BF16),
            pltpu.VMEM((4, 2, CHUNK, HEAD), BF16),
            pltpu.VMEM((4, 4, 2, *tile), BF16),
            pltpu.VMEM((16, 2, *tile), BF16),
            pltpu.VMEM((BLOCK + 8, 1024), F32),
            pltpu.VMEM((8, 2, 8, 128), F32),
            pltpu.VMEM((4, 2, 8, 128), F32),
            pltpu.VMEM((BLOCK, 1024), BF16),
            pltpu.VMEM((BLOCK, 1024), BF16),
            pltpu.VMEM((BLOCK, 1024), BF16),
            pltpu.VMEM((16, CHUNK, CHUNK), BF16),
            pltpu.VMEM((16, 1, CHUNK), F32),
            dma((8,)), dma, dma((4,)), dma,
            dma((5,)),
            dma((16,)), dma, dma((4,)), dma((4,)),
            dma((16,)), dma((8,)), dma((8,)), dma((8,)), dma((4,)), dma, dma((8,)), dma((16,)), dma((8,)),
            dma((2,)),
            dma((16,)), dma, dma, dma, dma, dma, dma, dma, dma, dma((2,)),
        ],
        compiler_params=pltpu.CompilerParams(collective_id=0, has_side_effects=True, vmem_limit_bytes=56 * 1024 * 1024),
        name="hyena",
    )(
        queries, key_rows, value_rows, gate_in, gate_out, kernel_taps.T, norm_gain.reshape(1, -1), cotangent
    )
    mixed, gq, gk, gv, ggi, ggo, gf, gg = pl.pallas_call(
        handed_on,
        out_shape=[jax.ShapeDtypeStruct(o.shape, o.dtype) for o in outs],
        in_specs=[hbm] * 8,
        out_specs=[hbm] * 8,
        scratch_shapes=[pltpu.VMEM(o.shape, o.dtype) for o in outs] + [dma((8,)), dma((8,))],
        name="results",
    )(*outs)
    return mixed, gq, gk, gv, ggi, ggo, gf.T, gg.reshape(-1)


def solution(mesh):
    wide = P("ctx", "chan")
    thin = (P("chan", None), P("chan"))
    return jax.shard_map(
        shards, mesh=mesh, in_specs=(wide,) * 5 + thin + (wide,), out_specs=(wide,) * 6 + thin, check_vma=False
    )
```

```python
import functools
import math

import jax
import jax.numpy as jnp
from jax import lax
from jax.experimental import pallas as pl
from jax.experimental.pallas import tpu as pltpu
from jax.sharding import PartitionSpec as P

HEAD = 128
FILT = 7
WIDTH = 4096
EPS = 1e-06
NEG = -1e30
SCALE = HEAD ** (-0.5)
SCALE2 = SCALE * math.log2(math.e)
BLOCK = 128
CHUNK = 512
F32 = jnp.float32
BF16 = jnp.bfloat16


def dot(a, b, ca, cb, precision=None):
    return lax.dot_general(
        a, b, (((ca,), (cb,)), ((), ())), preferred_element_type=F32, precision=precision
    )


def kernel(
    q_any, k_any, v_any, gi_any, go_any, taps_ref, gain_ref, cot_any,
    mixed_ref, gq_ref, gk_ref, gv_ref, ggi_ref, ggo_ref, gf_ref, gg_ref,
    kvs, qs, ssrc, kvb, qb, sb, du, dz, ot, lse2, osrc, ob, sum_sets, sum_heads, tot, hst,
    dqs, dqb, f_top, f_norm, dq_acc, d_out_t, d_rows, delta, kv_acc, sibs, sibb, dkvs, dkvb, zx, g_near, g_far,
    gi_ref, go_ref, cot_ref, wbuf, tops, su_send, su_recv, gx_send, gx_recv, in_sem, relay_send, relay_recv, sib_send, sib_recv,
    kv_send, q_send, s_send, o_send, st_send, h_send, dq_send, dkv_send, g_send, rim_send,
    kv_recv, q_recv, s_recv, o_recv, st_recv, h_recv, dq_recv, dkv_recv, g_recv, rim_recv,
):
    p = lax.axis_index("ctx")
    chan = lax.axis_index("chan")
    zh, core = chan // 2, chan % 2
    x, z, y = p // 8, (p // 4) % 2, p % 4
    hl0, m0 = x * 2 + y // 2, (x + y) % 2
    host = hl0 * 2 + m0
    home_chan = zh * 2 + z
    r0 = m0 * 2 + core

    def place(bit, e):
        return (e // 4) * 8 + bit * 4 + e % 4

    def chip(bit, e):
        return (e // 4) * 8 + bit * 4 + ((e // 2) % 2) * 2 + (e % 2 + e // 4) % 2

    def send(src, dst, send_sem, recv_sem, p2, chan2):
        own = jnp.logical_and(p2 == p, chan2 == chan)

        @pl.when(own)
        def _():
            pltpu.make_async_copy(src, dst, recv_sem).start()

        @pl.when(jnp.logical_not(own))
        def _():
            pltpu.make_async_remote_copy(
                src_ref=src, dst_ref=dst, send_sem=send_sem, recv_sem=recv_sem,
                device_id={"ctx": p2, "chan": chan2}, device_id_type=pl.DeviceIdType.MESH,
            ).start()

    def sent(src, dst, send_sem, recv_sem, p2, chan2):
        own = jnp.logical_and(p2 == p, chan2 == chan)

        @pl.when(jnp.logical_not(own))
        def _():
            pltpu.make_async_remote_copy(
                src_ref=src, dst_ref=dst, send_sem=send_sem, recv_sem=recv_sem,
                device_id={"ctx": p2, "chan": chan2}, device_id_type=pl.DeviceIdType.MESH,
            ).wait_send()

    def arrived(buf, recv_sem):
        pltpu.make_async_copy(buf, buf, recv_sem).wait()

    def moved(i, sign):
        step = (i * 5) % 16
        return ((x + sign * (step // 4) + 4) % 4) * 4 + (y + sign * (step % 4) + 4) % 4

    def kv_plan(i):
        e = moved(i, 1)
        return (
            kvs.at[e // 2], kvb.at[p], kv_send.at[i], kv_recv.at[p // 2],
            place(core, e), zh * 2 + p % 2,
        )

    def relay_source(i):
        return place(i % 2, moved(i - i % 2 + (y + core) % 2, -1))

    def relay_plan(i):
        source = relay_source(i)
        return (
            kvb.at[source], kvb.at[source], relay_send.at[i], relay_recv,
            p, zh * 2 + 1 - core, kv_recv.at[source // 2],
        )

    last_chunk = 7 - 2 * m0

    def kv_wanted(i, act):
        @pl.when(jnp.logical_or(own_chunk <= 5, ((i * 5 // 4) + i + x + y) % 2 == 0))
        def _():
            act(*kv_plan(i))

    def relay_wanted(i, act):
        @pl.when(relay_source(i) // 4 <= last_chunk)
        def _():
            act(*relay_plan(i))

    def loop(count, act, first=0):
        lax.fori_loop(first, count, lambda i, _: (act(i), 0)[1], 0)

    own_chunk = p // 4

    def relay(block, dst, send_sem, recv_sem, p2, chan2, landed):
        arrived(block, landed)
        send(block, dst, send_sem, recv_sem, p2, chan2)

    own_r = jnp.minimum(own_chunk, 7 - own_chunk)
    own_slot = (own_chunk // 4) * 4 + p % 4

    def q_plan(i):
        hl = (hl0 + 3 * i) % 8
        return (
            qs.at[hl], qb.at[own_slot], q_send.at[i], q_recv,
            chip(core, hl * 2 + own_r // 2), zh * 2 + own_r % 2,
        )

    def s_plan(i):
        hl = (hl0 + 3 * i) % 8
        return (
            ssrc.at[hl], sb.at[own_slot], s_send.at[i], s_recv,
            chip(core, hl * 2 + own_r // 2), zh * 2 + own_r % 2,
        )

    def slot_home(slot):
        return jnp.where(slot < 4, r0 * 4 + slot, (7 - r0) * 4 + slot - 4)

    def o_plan(i):
        slot = ((i + x) % 2) * 4 + (y + i // 2) % 4
        return osrc.at[slot], ob.at[hl0], o_send.at[i], o_recv, slot_home(slot), home_chan

    def dq_plan(i):
        slot = ((i + x) % 2) * 4 + (y + i // 2) % 4
        return dqs.at[slot], dqb.at[hl0], dq_send.at[i], dq_recv, slot_home(slot), home_chan

    def dkv_plan(i):
        return (
            dkvs.at[i // 4, i % 4], dkvb.at[m0 * 8 + hl0], dkv_send.at[i], dkv_recv,
            ((i // 4) * 2 + core) * 4 + i % 4, home_chan,
        )

    def sib_copy(i):
        return pltpu.make_async_remote_copy(
            src_ref=sibs.at[i], dst_ref=sibb.at[i], send_sem=sib_send.at[i], recv_sem=sib_recv.at[i],
            device_id={"ctx": p, "chan": zh * 2 + 1 - core}, device_id_type=pl.DeviceIdType.MESH,
        )

    def sib_sent(i):
        @pl.when(i * 2 + 1 - core <= 7 - r0)
        def _():
            sib_copy(i).wait_send()

    def dkv_sent(i):
        @pl.when((i // 4) * 2 + core <= last_chunk)
        def _():
            sent(*dkv_plan(i))

    def st_plan(i):
        g = (home_chan + i) % 4
        return (
            sum_sets.at[home_chan], sum_sets.at[home_chan], st_send.at[i], st_recv,
            chip(g % 2, host), (g // 2) * 2 + core,
        )

    def su_plan(i):
        hl = (hl0 + i) % 8
        return (
            sum_heads.at[hl0], sum_heads.at[hl0], su_send.at[i], su_recv,
            chip(z, hl * 2 + m0), chan,
        )

    def g_plan(i):
        g = (z * 4 + y + i) % 8
        return g_near.at[z * 4 + y], g_near.at[z * 4 + y], g_send.at[i], g_recv, x * 8 + g, chan

    def gx_plan(i):
        return g_far.at[x], g_far.at[x], gx_send.at[i], gx_recv, ((x + i) % 4) * 8 + z * 4 + y, chan

    def each(plan, count, act, first=0):
        lax.fori_loop(first, count, lambda i, _: (act(*plan(i)), 0)[1], 0)

    barrier = pltpu.get_barrier_semaphore()

    def greet(i, _):
        pl.semaphore_signal(
            barrier, inc=1, device_id={"ctx": (p + i // 2) % 32, "chan": zh * 2 + (core + i) % 2},
            device_id_type=pl.DeviceIdType.MESH,
        )
        return 0

    def greet_far(i, _):
        pl.semaphore_signal(
            barrier, inc=1, device_id={"ctx": chip(i, host), "chan": (1 - zh) * 2 + core},
            device_id_type=pl.DeviceIdType.MESH,
        )
        return 0

    lax.fori_loop(1, 64, greet, 0)
    lax.fori_loop(0, 2, greet_far, 0)
    wide_in = [
        pltpu.make_async_copy(src, dst, in_sem.at[j])
        for j, (src, dst) in enumerate(((cot_any, cot_ref), (go_any, go_ref), (gi_any, gi_ref)))
    ]
    for copy in wide_in:
        copy.start()
    for hl in range(8):
        cols = slice(hl * HEAD, (hl + 1) * HEAD)
        pltpu.make_async_copy(k_any.at[:, cols], kvs.at[hl, 0], in_sem.at[3]).start()
        pltpu.make_async_copy(v_any.at[:, cols], kvs.at[hl, 1], in_sem.at[3]).start()
        pltpu.make_async_copy(q_any.at[:, cols], qs.at[hl], in_sem.at[4]).start()
    wide_in[0].wait()
    wide_in[1].wait()
    du[pl.ds(0, BLOCK), :] = cot_ref[...].astype(F32) * go_ref[...].astype(F32)

    def rim_copy(src, dst, j, p2):
        return pltpu.make_async_remote_copy(
            src_ref=src, dst_ref=dst, send_sem=rim_send.at[j], recv_sem=rim_recv.at[j],
            device_id={"ctx": p2, "chan": chan}, device_id_type=pl.DeviceIdType.MESH,
        )

    du_rim = rim_copy(du.at[pl.ds(0, 8)], du.at[pl.ds(BLOCK, 8)], 0, jnp.maximum(p - 1, 0))
    z_rim = rim_copy(zx.at[pl.ds(BLOCK, 8)], zx.at[pl.ds(0, 8)], 1, jnp.minimum(p + 1, 31))

    group_of = lax.broadcasted_iota(jnp.int32, (128, 1024), 1) // 8
    spread = (group_of == lax.broadcasted_iota(jnp.int32, (128, 1024), 0)).astype(F32)
    taps = dot(taps_ref[...], spread, 1, 0, lax.Precision.HIGHEST)
    gain = gain_ref[...]

    pltpu.make_async_copy(kvs, kvs, in_sem.at[3]).wait()
    pltpu.make_async_copy(qs, qs, in_sem.at[4]).wait()
    wide_in[2].wait()
    pl.semaphore_wait(barrier, 65)

    @pl.when(p > 0)
    def _():
        du_rim.start()

    each(q_plan, 8, send)
    loop(16, lambda i: kv_wanted(i, send))

    @pl.when(p == 31)
    def _():
        du[pl.ds(BLOCK, 8), :] = jnp.zeros((8, 1024), F32)

    @pl.when(p < 31)
    def _():
        du_rim.wait_recv()

    for hl in range(8):
        cols = slice(hl * HEAD, (hl + 1) * HEAD)
        total = taps[0:1, cols] * du[pl.ds(0, BLOCK), cols]
        for lag in range(1, FILT):
            total = total + taps[lag : lag + 1, cols] * du[pl.ds(lag, BLOCK), cols]
        dz[:, cols] = total
        ssrc[hl] = (total * gi_ref[:, cols].astype(F32) * gain[:, cols]).astype(BF16)

    below = lax.broadcasted_iota(jnp.int32, (CHUNK, CHUNK), 0) <= lax.broadcasted_iota(
        jnp.int32, (CHUNK, CHUNK), 1
    )

    def keys_of(kt):
        return kvb[pl.ds(kt * 4, 4), 0].reshape(CHUNK, HEAD)

    def values_of(kt):
        return kvb[pl.ds(kt * 4, 4), 1].reshape(CHUNK, HEAD)

    chunks = (r0, 7 - r0)
    f_top[...] = jnp.full((1, 1024), NEG, F32)
    f_norm[...] = jnp.zeros((1, 1024), F32)
    ot[...] = jnp.zeros((HEAD, 1024), F32)

    def forward(qc, kt, masked):
        rows = slice(qc * CHUNK, (qc + 1) * CHUNK)
        s = dot(keys_of(kt), qb[pl.ds(qc * 4, 4)].reshape(CHUNK, HEAD), 1, 1)
        if masked:
            s = jnp.where(below, s, NEG)
        top = f_top[:, rows]
        new_top = jnp.maximum(top, jnp.max(s, axis=0, keepdims=True))
        w = jnp.exp2(s * SCALE2 - new_top * SCALE2)
        w_low = w.astype(BF16)
        wbuf[qc * 8 + kt] = w_low
        tops[qc * 8 + kt] = new_top
        fade = jnp.exp2((top - new_top) * SCALE2)
        f_top[:, rows] = new_top
        f_norm[:, rows] = f_norm[:, rows] * fade + jnp.sum(w, axis=0, keepdims=True)
        ot[:, rows] = ot[:, rows] * fade + dot(values_of(kt), w_low, 0, 0)

    def forward_chunk(kt, _):
        for qc in range(2):

            @pl.when(kt < chunks[qc])
            def _():
                forward(qc, kt, False)

            @pl.when(kt == chunks[qc])
            def _():
                forward(qc, kt, True)

        return 0

    loop(16, lambda i: relay_wanted(i, relay))
    each(s_plan, 8, send)

    @pl.when(m0 == 0)
    def _():
        arrived(kvb.at[pl.ds(0, 16)], relay_recv)

    @pl.when(m0 == 1)
    def _():
        arrived(kvb.at[pl.ds(0, 12)], relay_recv)

    arrived(qb, q_recv)
    lax.fori_loop(0, 8, forward_chunk, 0)
    arrived(sb, s_recv)
    for qc in range(2):
        rows = slice(qc * CHUNK, (qc + 1) * CHUNK)
        norm = f_norm[:, rows]
        out = (ot[:, rows] * (1.0 / norm)).astype(BF16)
        out_wide = out.astype(F32)
        ot[:, rows] = out_wide
        lse2[:, rows] = f_top[:, rows] * SCALE2 + jnp.log2(norm)
        osrc[pl.ds(qc * 4, 4)] = out_wide.T.astype(BF16).reshape(4, HEAD, HEAD)
        s_t = sb[pl.ds(qc * 4, 4)].reshape(CHUNK, HEAD).astype(F32).T
        squares = jnp.sum(out_wide * out_wide, axis=0, keepdims=True)
        dots = jnp.sum(s_t * out_wide, axis=0, keepdims=True)
        for j in range(4):
            at = slice(j * HEAD, (j + 1) * HEAD)
            sum_sets[home_chan, 0, qc * 4 + j : qc * 4 + j + 1, :] = squares[:, at]
            sum_sets[home_chan, 1, qc * 4 + j : qc * 4 + j + 1, :] = dots[:, at]

    each(st_plan, 4, send, 1)
    arrived(sum_sets.at[pl.ds(0, 3)], st_recv)
    sum_heads[hl0] = jnp.sum(sum_sets[...], axis=0)
    each(su_plan, 8, send, 1)
    each(o_plan, 8, send)
    arrived(sum_heads.at[pl.ds(0, 7)], su_recv)
    tot[...] = jnp.sum(sum_heads[...], axis=0)
    home_slot = jnp.where(r0 % 2 == hl0 // 4, hl0 % 4, 4 + hl0 % 4)
    h_args = (tot, hst, h_send, h_recv, slot_home(home_slot), home_chan)
    send(*h_args)

    rstd_all = lax.rsqrt(tot[0] / WIDTH + EPS)
    drop_all = rstd_all * rstd_all * rstd_all * tot[1] / WIDTH

    for qc in range(2):
        rows = slice(qc * CHUNK, (qc + 1) * CHUNK)
        s_t = sb[pl.ds(qc * 4, 4)].reshape(CHUNK, HEAD).astype(F32).T
        out_wide = ot[:, rows]

        def lanes(a, qc=qc):
            return jnp.concatenate([a[qc * 4 + j : qc * 4 + j + 1] for j in range(4)], axis=1)

        d_low = (lanes(rstd_all) * s_t - out_wide * lanes(drop_all)).astype(BF16)
        d_wide = d_low.astype(F32)
        delta[:, rows] = jnp.sum(d_wide * out_wide, axis=0, keepdims=True)
        d_out_t[:, rows] = d_low
        d_rows[rows, :] = d_wide.T.astype(BF16)
        dq_acc[:, rows] = jnp.zeros((HEAD, CHUNK), F32)

    def backward(qc, kt, slot):
        rows = slice(qc * CHUNK, (qc + 1) * CHUNK)
        q_rows = qb[pl.ds(qc * 4, 4)].reshape(CHUNK, HEAD)
        k_rows = keys_of(kt)
        w = wbuf[qc * 8 + kt].astype(F32) * jnp.exp2(tops[qc * 8 + kt] * SCALE2 - lse2[:, rows])
        d_w = dot(values_of(kt), d_out_t[:, rows], 1, 0)
        d_s = (w * (d_w - delta[:, rows])).astype(BF16)
        d_k = dot(d_s, q_rows, 1, 0)
        d_v = dot(w.astype(BF16), d_rows[rows, :], 1, 0)
        dq_acc[:, rows] += dot(k_rows, d_s, 0, 0)
        if qc == 1:
            kv_acc[slot, 0] = d_k
            kv_acc[slot, 1] = d_v
        else:
            kv_acc[slot, 0] += d_k
            kv_acc[slot, 1] += d_v

    def finish(kt, slot):
        @pl.when(jnp.logical_and(kt % 2 == core, kt <= last_chunk))
        def _():
            sib_copy(kt // 2).wait_recv()
            for which, scale in ((0, SCALE), (1, 1.0)):
                both = kv_acc[slot, which] * scale + sibb[kt // 2, which].astype(F32)
                dkvs[kt // 2, :, which] = both.astype(BF16).reshape(4, HEAD, HEAD)
            loop((kt // 2) * 4 + 4, lambda i: send(*dkv_plan(i)), (kt // 2) * 4)

    first = hl0 + 2 * y

    def key_chunk(t, _):
        kt, slot = (first + t) % 8, t % 2
        for qc in (1, 0):
            @pl.when(kt <= chunks[qc])
            def _():
                backward(qc, kt, slot)

        @pl.when(jnp.logical_and(kt % 2 != core, kt <= 7 - r0))
        def _():
            for which, scale in ((0, SCALE), (1, 1.0)):
                sibs[kt // 2, which] = (kv_acc[slot, which] * scale).astype(BF16)
            sib_copy(kt // 2).start()

        @pl.when(jnp.logical_and(kt % 2 == core, kt > 7 - r0))
        def _():
            kv_acc[slot] = jnp.zeros((2, CHUNK, HEAD), F32)

        @pl.when(t > 0)
        def _():
            finish((kt + 7) % 8, 1 - slot)

        return 0

    lax.fori_loop(0, 4, key_chunk, 0)
    arrived(ob, o_recv)
    arrived(hst, h_recv)
    square_row = hst[0, pl.ds(own_slot, 1), :]
    rstd_row = lax.rsqrt(square_row / WIDTH + EPS)
    rstd = jnp.broadcast_to(rstd_row, (BLOCK, BLOCK)).T
    for hl in range(8):
        cols = slice(hl * HEAD, (hl + 1) * HEAD)
        a_hat = ob[hl].astype(F32) * rstd
        normed = a_hat * gain[:, cols]
        gate = gi_ref[:, cols].astype(F32)
        zx[pl.ds(8, BLOCK), cols] = gate * normed
        ggi_ref[:, cols] = (dz[:, cols] * normed).astype(BF16)
        g_near[z * 4 + y, 1, hl : hl + 1, :] = jnp.sum(dz[:, cols] * gate * a_hat, axis=0, keepdims=True)

    @pl.when(p < 31)
    def _():
        z_rim.start()

    @pl.when(p == 0)
    def _():
        zx[pl.ds(0, 8), :] = jnp.zeros((8, 1024), F32)

    lax.fori_loop(4, 6, key_chunk, 0)
    @pl.when(p > 0)
    def _():
        z_rim.wait_recv()

    tap_sums = []
    for hl in range(8):
        cols = slice(hl * HEAD, (hl + 1) * HEAD)
        d_conv = du[pl.ds(0, BLOCK), cols]
        conv = jnp.zeros((BLOCK, HEAD), F32)
        sums = []
        for lag in range(FILT):
            shifted = zx[pl.ds(8 - lag, BLOCK), cols]
            conv = conv + taps[lag : lag + 1, cols] * shifted
            sums.append(jnp.sum(d_conv * shifted, axis=0, keepdims=True))
        sums.append(jnp.zeros((1, HEAD), F32))
        tap_sums.append(jnp.concatenate(sums, axis=0))
        mixed_ref[:, cols] = (go_ref[:, cols].astype(F32) * conv).astype(BF16)
        ggo_ref[:, cols] = (cot_ref[:, cols].astype(F32) * conv).astype(BF16)
    g_near[z * 4 + y, 0] = dot(jnp.concatenate(tap_sums, axis=1), spread, 1, 1, lax.Precision.HIGHEST)
    each(g_plan, 8, send, 1)
    lax.fori_loop(6, 8, key_chunk, 0)
    finish((first + 7) % 8, 1)
    for qc in range(2):
        dq = dq_acc[:, qc * CHUNK : (qc + 1) * CHUNK] * SCALE
        dqs[pl.ds(qc * 4, 4)] = dq.T.astype(BF16).reshape(4, HEAD, HEAD)
    each(dq_plan, 8, send)
    arrived(g_near.at[pl.ds(0, 7)], g_recv)
    g_far[x] = jnp.sum(g_near[...], axis=0)
    each(gx_plan, 4, send, 1)
    each(o_plan, 8, sent)
    sent(*h_args)
    each(su_plan, 8, sent, 1)
    each(g_plan, 8, sent, 1)
    arrived(g_far.at[pl.ds(0, 3)], gx_recv)
    g_total = jnp.sum(g_far[...], axis=0)
    gf_ref[...] = g_total[0, :FILT]
    gg_ref[...] = g_total[1]
    loop(16, lambda i: kv_wanted(i, sent))
    each(q_plan, 8, sent)
    loop(16, lambda i: relay_wanted(i, lambda *a: sent(*a[:6])))
    each(st_plan, 4, sent, 1)
    each(s_plan, 8, sent)
    lax.fori_loop(0, 4, lambda i, _: (sib_sent(i), 0)[1], 0)
    lax.fori_loop(0, 16, lambda i, _: (dkv_sent(i), 0)[1], 0)
    each(dq_plan, 8, sent)
    each(gx_plan, 4, sent, 1)

    @pl.when(p > 0)
    def _():
        du_rim.wait_send()

    @pl.when(p < 31)
    def _():
        z_rim.wait_send()

    arrived(dqb, dq_recv)

    def all_keys(parts):
        arrived(dkvb.at[pl.ds(0, parts * 8)], dkv_recv)
        for hl in range(8):
            cols = slice(hl * HEAD, (hl + 1) * HEAD)
            for which, out_ref in ((0, gk_ref), (1, gv_ref)):
                total = dkvb[hl, which]
                if parts == 2:
                    total = (total.astype(F32) + dkvb[8 + hl, which].astype(F32)).astype(BF16)
                out_ref[:, cols] = total

    for hl in range(8):
        gq_ref[:, hl * HEAD : (hl + 1) * HEAD] = dqb[hl]

    @pl.when(own_chunk <= 5)
    def _():
        all_keys(2)

    @pl.when(own_chunk > 5)
    def _():
        all_keys(1)


def handed_on(*refs):
    held, in_sem, out_sem = refs[16:24], refs[24], refs[25]
    loads = [pltpu.make_async_copy(refs[i], held[i], in_sem.at[i]) for i in range(8)]
    stores = [pltpu.make_async_copy(held[i], refs[8 + i], out_sem.at[i]) for i in range(8)]
    for load in loads:
        load.start()
    for load, store in zip(loads, stores):
        load.wait()
        store.start()
    for store in stores:
        store.wait()


def shards(queries, key_rows, value_rows, gate_in, gate_out, kernel_taps, norm_gain, cotangent):
    rows = jax.ShapeDtypeStruct((BLOCK, 1024), BF16)
    vmem = pl.BlockSpec(memory_space=pltpu.VMEM)
    hbm = pl.BlockSpec(memory_space=pl.ANY)
    tile = (HEAD, HEAD)
    dma = pltpu.SemaphoreType.DMA
    outs = pl.pallas_call(
        kernel,
        out_shape=[rows] * 6 + [jax.ShapeDtypeStruct((FILT, 128), F32), jax.ShapeDtypeStruct((8, 128), F32)],
        in_specs=[hbm] * 5 + [vmem] * 2 + [hbm],
        out_specs=[vmem] * 8,
        scratch_shapes=[
            pltpu.VMEM((8, 2, *tile), BF16),
            pltpu.VMEM((8, *tile), BF16),
            pltpu.VMEM((8, *tile), BF16),
            pltpu.VMEM((32, 2, *tile), BF16),
            pltpu.VMEM((8, *tile), BF16),
            pltpu.VMEM((8, *tile), BF16),
            pltpu.VMEM((BLOCK + 8, 1024), F32),
            pltpu.VMEM((BLOCK, 1024), F32),
            pltpu.VMEM((HEAD, 1024), F32),
            pltpu.VMEM((1, 1024), F32),
            pltpu.VMEM((8, *tile), BF16),
            pltpu.VMEM((8, *tile), BF16),
            pltpu.VMEM((4, 2, 8, 128), F32),
            pltpu.VMEM((8, 2, 8, 128), F32),
            pltpu.VMEM((2, 8, 128), F32),
            pltpu.VMEM((2, 8, 128), F32),
            pltpu.VMEM((8, *tile), BF16),
            pltpu.VMEM((8, *tile), BF16),
            pltpu.VMEM((1, 1024), F32),
            pltpu.VMEM((1, 1024), F32),
            pltpu.VMEM((HEAD, 1024), F32),
            pltpu.VMEM((HEAD, 1024), BF16),
            pltpu.VMEM((1024, HEAD), BF16),
            pltpu.VMEM((1, 1024), F32),
            pltpu.VMEM((2, 2, CHUNK, HEAD), F32),
            pltpu.VMEM((4, 2, CHUNK, HEAD), BF16),
            pltpu.VMEM((4, 2, CHUNK, HEAD), BF16),
            pltpu.VMEM((4, 4, 2, *tile), BF16),
            pltpu.VMEM((16, 2, *tile), BF16),
            pltpu.VMEM((BLOCK + 8, 1024), F32),
            pltpu.VMEM((8, 2, 8, 128), F32),
            pltpu.VMEM((4, 2, 8, 128), F32),
            pltpu.VMEM((BLOCK, 1024), BF16),
            pltpu.VMEM((BLOCK, 1024), BF16),
            pltpu.VMEM((BLOCK, 1024), BF16),
            pltpu.VMEM((16, CHUNK, CHUNK), BF16),
            pltpu.VMEM((16, 1, CHUNK), F32),
            dma((8,)), dma, dma((4,)), dma,
            dma((5,)),
            dma((16,)), dma, dma((4,)), dma((4,)),
            dma((16,)), dma((8,)), dma((8,)), dma((8,)), dma((4,)), dma, dma((8,)), dma((16,)), dma((8,)),
            dma((2,)),
            dma((16,)), dma, dma, dma, dma, dma, dma, dma, dma, dma((2,)),
        ],
        compiler_params=pltpu.CompilerParams(collective_id=0, has_side_effects=True, vmem_limit_bytes=56 * 1024 * 1024),
        name="hyena",
    )(
        queries, key_rows, value_rows, gate_in, gate_out, kernel_taps.T, norm_gain.reshape(1, -1), cotangent
    )
    mixed, gq, gk, gv, ggi, ggo, gf, gg = pl.pallas_call(
        handed_on,
        out_shape=[jax.ShapeDtypeStruct(o.shape, o.dtype) for o in outs],
        in_specs=[hbm] * 8,
        out_specs=[hbm] * 8,
        scratch_shapes=[pltpu.VMEM(o.shape, o.dtype) for o in outs] + [dma((8,)), dma((8,))],
        name="results",
    )(*outs)
    return mixed, gq, gk, gv, ggi, ggo, gf.T, gg.reshape(-1)


def solution(mesh):
    wide = P("ctx", "chan")
    thin = (P("chan", None), P("chan"))
    return jax.shard_map(
        shards, mesh=mesh, in_specs=(wide,) * 5 + thin + (wide,), out_specs=(wide,) * 6 + thin, check_vma=False
    )
```

```python
import functools
import math

import jax
import jax.numpy as jnp
from jax import lax
from jax.experimental import pallas as pl
from jax.experimental.pallas import tpu as pltpu
from jax.sharding import PartitionSpec as P

HEAD = 128
FILT = 7
WIDTH = 4096
EPS = 1e-06
NEG = -1e30
SCALE = HEAD ** (-0.5)
SCALE2 = SCALE * math.log2(math.e)
BLOCK = 128
CHUNK = 512
F32 = jnp.float32
BF16 = jnp.bfloat16


def dot(a, b, ca, cb, precision=None):
    return lax.dot_general(
        a, b, (((ca,), (cb,)), ((), ())), preferred_element_type=F32, precision=precision
    )


def kernel(
    q_any, k_any, v_any, gi_any, go_any, taps_ref, gain_ref, cot_any,
    mixed_ref, gq_ref, gk_ref, gv_ref, ggi_ref, ggo_ref, gf_ref, gg_ref,
    kvs, qs, ssrc, kvb, qb, sb, du, dz, ot, lse2, osrc, ob, sum_sets, sum_heads, tot, hst,
    dqs, dqb, f_top, f_norm, s_keep, dq_acc, d_out_t, d_rows, delta, kv_acc, sibs, sibb, dkvs, dkvb, zx, g_near, g_far,
    gi_ref, go_ref, cot_ref, wbuf, tops, su_send, su_recv, gx_send, gx_recv, in_sem, relay_send, relay_recv, sib_send, sib_recv,
    kv_send, q_send, s_send, o_send, st_send, h_send, dq_send, dkv_send, g_send, rim_send,
    kv_recv, q_recv, s_recv, o_recv, st_recv, h_recv, dq_recv, dkv_recv, g_recv, rim_recv,
):
    p = lax.axis_index("ctx")
    chan = lax.axis_index("chan")
    zh, core = chan // 2, chan % 2
    x, z, y = p // 8, (p // 4) % 2, p % 4
    hl0, m0 = x * 2 + y // 2, (x + y) % 2
    host = hl0 * 2 + m0
    home_chan = zh * 2 + z
    r0 = m0 * 2 + core

    def place(bit, e):
        return (e // 4) * 8 + bit * 4 + e % 4

    def chip(bit, e):
        return (e // 4) * 8 + bit * 4 + ((e // 2) % 2) * 2 + (e % 2 + e // 4) % 2

    def send(src, dst, send_sem, recv_sem, p2, chan2):
        own = jnp.logical_and(p2 == p, chan2 == chan)

        @pl.when(own)
        def _():
            pltpu.make_async_copy(src, dst, recv_sem).start()

        @pl.when(jnp.logical_not(own))
        def _():
            pltpu.make_async_remote_copy(
                src_ref=src, dst_ref=dst, send_sem=send_sem, recv_sem=recv_sem,
                device_id={"ctx": p2, "chan": chan2}, device_id_type=pl.DeviceIdType.MESH,
            ).start()

    def sent(src, dst, send_sem, recv_sem, p2, chan2):
        own = jnp.logical_and(p2 == p, chan2 == chan)

        @pl.when(jnp.logical_not(own))
        def _():
            pltpu.make_async_remote_copy(
                src_ref=src, dst_ref=dst, send_sem=send_sem, recv_sem=recv_sem,
                device_id={"ctx": p2, "chan": chan2}, device_id_type=pl.DeviceIdType.MESH,
            ).wait_send()

    def arrived(buf, recv_sem):
        pltpu.make_async_copy(buf, buf, recv_sem).wait()

    def moved(i, sign):
        step = (i * 5) % 16
        return ((x + sign * (step // 4) + 4) % 4) * 4 + (y + sign * (step % 4) + 4) % 4

    def kv_plan(i):
        e = moved(i, 1)
        return (
            kvs.at[e // 2], kvb.at[p], kv_send.at[i], kv_recv.at[p // 2],
            place(core, e), zh * 2 + p % 2,
        )

    def relay_source(i):
        return place(i % 2, moved(i - i % 2 + (y + core) % 2, -1))

    def relay_plan(i):
        source = relay_source(i)
        return (
            kvb.at[source], kvb.at[source], relay_send.at[i], relay_recv,
            p, zh * 2 + 1 - core, kv_recv.at[source // 2],
        )

    last_chunk = 7 - 2 * m0

    def kv_wanted(i, act):
        @pl.when(jnp.logical_or(own_chunk <= 5, ((i * 5 // 4) + i + x + y) % 2 == 0))
        def _():
            act(*kv_plan(i))

    def relay_wanted(i, act):
        @pl.when(relay_source(i) // 4 <= last_chunk)
        def _():
            act(*relay_plan(i))

    def loop(count, act, first=0):
        lax.fori_loop(first, count, lambda i, _: (act(i), 0)[1], 0)

    own_chunk = p // 4

    def relay(block, dst, send_sem, recv_sem, p2, chan2, landed):
        arrived(block, landed)
        send(block, dst, send_sem, recv_sem, p2, chan2)

    own_r = jnp.minimum(own_chunk, 7 - own_chunk)
    own_slot = (own_chunk // 4) * 4 + p % 4

    def q_plan(i):
        hl = (hl0 + 3 * i) % 8
        return (
            qs.at[hl], qb.at[own_slot], q_send.at[i], q_recv,
            chip(core, hl * 2 + own_r // 2), zh * 2 + own_r % 2,
        )

    def s_plan(i):
        hl = (hl0 + 3 * i) % 8
        return (
            ssrc.at[hl], sb.at[own_slot], s_send.at[i], s_recv,
            chip(core, hl * 2 + own_r // 2), zh * 2 + own_r % 2,
        )

    def slot_home(slot):
        return jnp.where(slot < 4, r0 * 4 + slot, (7 - r0) * 4 + slot - 4)

    def o_plan(i):
        slot = ((i + x) % 2) * 4 + (y + i // 2) % 4
        return osrc.at[slot], ob.at[hl0], o_send.at[i], o_recv, slot_home(slot), home_chan

    def dq_plan(i):
        slot = ((i + x) % 2) * 4 + (y + i // 2) % 4
        return dqs.at[slot], dqb.at[hl0], dq_send.at[i], dq_recv, slot_home(slot), home_chan

    def dkv_plan(i):
        return (
            dkvs.at[i // 4, i % 4], dkvb.at[m0 * 8 + hl0], dkv_send.at[i], dkv_recv,
            ((i // 4) * 2 + core) * 4 + i % 4, home_chan,
        )

    def sib_copy(i):
        return pltpu.make_async_remote_copy(
            src_ref=sibs.at[i], dst_ref=sibb.at[i], send_sem=sib_send.at[i], recv_sem=sib_recv.at[i],
            device_id={"ctx": p, "chan": zh * 2 + 1 - core}, device_id_type=pl.DeviceIdType.MESH,
        )

    def sib_sent(i):
        @pl.when(i * 2 + 1 - core <= 7 - r0)
        def _():
            sib_copy(i).wait_send()

    def dkv_sent(i):
        @pl.when((i // 4) * 2 + core <= last_chunk)
        def _():
            sent(*dkv_plan(i))

    def st_plan(i):
        g = (home_chan + i) % 4
        return (
            sum_sets.at[home_chan], sum_sets.at[home_chan], st_send.at[i], st_recv,
            chip(g % 2, host), (g // 2) * 2 + core,
        )

    def su_plan(i):
        hl = (hl0 + i) % 8
        return (
            sum_heads.at[hl0], sum_heads.at[hl0], su_send.at[i], su_recv,
            chip(z, hl * 2 + m0), chan,
        )

    def g_plan(i):
        g = (z * 4 + y + i) % 8
        return g_near.at[z * 4 + y], g_near.at[z * 4 + y], g_send.at[i], g_recv, x * 8 + g, chan

    def gx_plan(i):
        return g_far.at[x], g_far.at[x], gx_send.at[i], gx_recv, ((x + i) % 4) * 8 + z * 4 + y, chan

    def each(plan, count, act, first=0):
        lax.fori_loop(first, count, lambda i, _: (act(*plan(i)), 0)[1], 0)

    barrier = pltpu.get_barrier_semaphore()

    def greet(i, _):
        pl.semaphore_signal(
            barrier, inc=1, device_id={"ctx": (p + i // 2) % 32, "chan": zh * 2 + (core + i) % 2},
            device_id_type=pl.DeviceIdType.MESH,
        )
        return 0

    def greet_far(i, _):
        pl.semaphore_signal(
            barrier, inc=1, device_id={"ctx": chip(i, host), "chan": (1 - zh) * 2 + core},
            device_id_type=pl.DeviceIdType.MESH,
        )
        return 0

    lax.fori_loop(1, 64, greet, 0)
    lax.fori_loop(0, 2, greet_far, 0)
    wide_in = [
        pltpu.make_async_copy(src, dst, in_sem.at[j])
        for j, (src, dst) in enumerate(((cot_any, cot_ref), (go_any, go_ref), (gi_any, gi_ref)))
    ]
    for copy in wide_in:
        copy.start()
    for hl in range(8):
        cols = slice(hl * HEAD, (hl + 1) * HEAD)
        pltpu.make_async_copy(k_any.at[:, cols], kvs.at[hl, 0], in_sem.at[3]).start()
        pltpu.make_async_copy(v_any.at[:, cols], kvs.at[hl, 1], in_sem.at[3]).start()
        pltpu.make_async_copy(q_any.at[:, cols], qs.at[hl], in_sem.at[4]).start()
    wide_in[0].wait()
    wide_in[1].wait()
    du[pl.ds(0, BLOCK), :] = cot_ref[...].astype(F32) * go_ref[...].astype(F32)

    def rim_copy(src, dst, j, p2):
        return pltpu.make_async_remote_copy(
            src_ref=src, dst_ref=dst, send_sem=rim_send.at[j], recv_sem=rim_recv.at[j],
            device_id={"ctx": p2, "chan": chan}, device_id_type=pl.DeviceIdType.MESH,
        )

    du_rim = rim_copy(du.at[pl.ds(0, 8)], du.at[pl.ds(BLOCK, 8)], 0, jnp.maximum(p - 1, 0))
    z_rim = rim_copy(zx.at[pl.ds(BLOCK, 8)], zx.at[pl.ds(0, 8)], 1, jnp.minimum(p + 1, 31))

    group_of = lax.broadcasted_iota(jnp.int32, (128, 1024), 1) // 8
    spread = (group_of == lax.broadcasted_iota(jnp.int32, (128, 1024), 0)).astype(F32)
    taps = dot(taps_ref[...], spread, 1, 0, lax.Precision.HIGHEST)
    gain = gain_ref[...]

    pltpu.make_async_copy(kvs, kvs, in_sem.at[3]).wait()
    pltpu.make_async_copy(qs, qs, in_sem.at[4]).wait()
    wide_in[2].wait()
    pl.semaphore_wait(barrier, 65)

    @pl.when(p > 0)
    def _():
        du_rim.start()

    each(q_plan, 8, send)
    loop(16, lambda i: kv_wanted(i, send))

    @pl.when(p == 31)
    def _():
        du[pl.ds(BLOCK, 8), :] = jnp.zeros((8, 1024), F32)

    @pl.when(p < 31)
    def _():
        du_rim.wait_recv()

    for hl in range(8):
        cols = slice(hl * HEAD, (hl + 1) * HEAD)
        total = taps[0:1, cols] * du[pl.ds(0, BLOCK), cols]
        for lag in range(1, FILT):
            total = total + taps[lag : lag + 1, cols] * du[pl.ds(lag, BLOCK), cols]
        dz[:, cols] = total
        ssrc[hl] = (total * gi_ref[:, cols].astype(F32) * gain[:, cols]).astype(BF16)

    below = lax.broadcasted_iota(jnp.int32, (CHUNK, CHUNK), 0) <= lax.broadcasted_iota(
        jnp.int32, (CHUNK, CHUNK), 1
    )

    def keys_of(kt):
        return kvb[pl.ds(kt * 4, 4), 0].reshape(CHUNK, HEAD)

    def values_of(kt):
        return kvb[pl.ds(kt * 4, 4), 1].reshape(CHUNK, HEAD)

    chunks = (r0, 7 - r0)
    f_top[...] = jnp.full((1, 1024), NEG, F32)
    f_norm[...] = jnp.zeros((1, 1024), F32)
    ot[...] = jnp.zeros((HEAD, 1024), F32)

    def forward(qc, kt, masked):
        rows = slice(qc * CHUNK, (qc + 1) * CHUNK)
        s = dot(keys_of(kt), qb[pl.ds(qc * 4, 4)].reshape(CHUNK, HEAD), 1, 1)
        if masked:
            s = jnp.where(below, s, NEG)
        top = f_top[:, rows]
        new_top = jnp.maximum(top, jnp.max(s, axis=0, keepdims=True))
        w = jnp.exp2(s * SCALE2 - new_top * SCALE2)
        w_low = w.astype(BF16)
        wbuf[qc * 8 + kt] = w_low
        tops[qc * 8 + kt] = new_top
        fade = jnp.exp2((top - new_top) * SCALE2)
        f_top[:, rows] = new_top
        f_norm[:, rows] = f_norm[:, rows] * fade + jnp.sum(w, axis=0, keepdims=True)
        ot[:, rows] = ot[:, rows] * fade + dot(values_of(kt), w_low, 0, 0)

    def forward_chunk(kt, _):
        for qc in range(2):

            @pl.when(kt < chunks[qc])
            def _():
                forward(qc, kt, False)

            @pl.when(kt == chunks[qc])
            def _():
                forward(qc, kt, True)

        return 0

    loop(16, lambda i: relay_wanted(i, relay))
    each(s_plan, 8, send)

    @pl.when(m0 == 0)
    def _():
        arrived(kvb.at[pl.ds(0, 16)], relay_recv)

    @pl.when(m0 == 1)
    def _():
        arrived(kvb.at[pl.ds(0, 12)], relay_recv)

    arrived(qb, q_recv)
    lax.fori_loop(0, 8, forward_chunk, 0)
    arrived(sb, s_recv)
    for qc in range(2):
        rows = slice(qc * CHUNK, (qc + 1) * CHUNK)
        norm = f_norm[:, rows]
        out = (ot[:, rows] * (1.0 / norm)).astype(BF16)
        out_wide = out.astype(F32)
        ot[:, rows] = out_wide
        lse2[:, rows] = f_top[:, rows] * SCALE2 + jnp.log2(norm)
        s_t = sb[pl.ds(qc * 4, 4)].reshape(CHUNK, HEAD).astype(F32).T
        s_keep[:, rows] = s_t
        squares = jnp.sum(out_wide * out_wide, axis=0, keepdims=True)
        dots = jnp.sum(s_t * out_wide, axis=0, keepdims=True)
        for j in range(4):
            at = slice(j * HEAD, (j + 1) * HEAD)
            sum_sets[home_chan, 0, qc * 4 + j : qc * 4 + j + 1, :] = squares[:, at]
            sum_sets[home_chan, 1, qc * 4 + j : qc * 4 + j + 1, :] = dots[:, at]

    each(st_plan, 4, send, 1)
    for qc in range(2):
        out_wide = ot[:, qc * CHUNK : (qc + 1) * CHUNK]
        osrc[pl.ds(qc * 4, 4)] = out_wide.T.astype(BF16).reshape(4, HEAD, HEAD)
    arrived(sum_sets.at[pl.ds(0, 3)], st_recv)
    sum_heads[hl0] = jnp.sum(sum_sets[...], axis=0)
    each(su_plan, 8, send, 1)
    each(o_plan, 8, send)
    arrived(sum_heads.at[pl.ds(0, 7)], su_recv)
    tot[...] = jnp.sum(sum_heads[...], axis=0)
    home_slot = jnp.where(r0 % 2 == hl0 // 4, hl0 % 4, 4 + hl0 % 4)
    h_args = (tot, hst, h_send, h_recv, slot_home(home_slot), home_chan)
    send(*h_args)

    rstd_all = lax.rsqrt(tot[0] / WIDTH + EPS)
    drop_all = rstd_all * rstd_all * rstd_all * tot[1] / WIDTH

    for qc in range(2):
        rows = slice(qc * CHUNK, (qc + 1) * CHUNK)
        s_t = s_keep[:, rows]
        out_wide = ot[:, rows]

        def lanes(a, qc=qc):
            return jnp.concatenate([a[qc * 4 + j : qc * 4 + j + 1] for j in range(4)], axis=1)

        d_low = (lanes(rstd_all) * s_t - out_wide * lanes(drop_all)).astype(BF16)
        d_wide = d_low.astype(F32)
        delta[:, rows] = jnp.sum(d_wide * out_wide, axis=0, keepdims=True)
        d_out_t[:, rows] = d_low
        d_rows[rows, :] = d_wide.T.astype(BF16)
        dq_acc[:, rows] = jnp.zeros((HEAD, CHUNK), F32)

    def backward(qc, kt, slot):
        rows = slice(qc * CHUNK, (qc + 1) * CHUNK)
        q_rows = qb[pl.ds(qc * 4, 4)].reshape(CHUNK, HEAD)
        k_rows = keys_of(kt)
        w = wbuf[qc * 8 + kt].astype(F32) * jnp.exp2(tops[qc * 8 + kt] * SCALE2 - lse2[:, rows])
        d_w = dot(values_of(kt), d_out_t[:, rows], 1, 0)
        d_s = (w * (d_w - delta[:, rows])).astype(BF16)
        d_k = dot(d_s, q_rows, 1, 0)
        d_v = dot(w.astype(BF16), d_rows[rows, :], 1, 0)
        dq_acc[:, rows] += dot(k_rows, d_s, 0, 0)
        if qc == 1:
            kv_acc[slot, 0] = d_k
            kv_acc[slot, 1] = d_v
        else:
            kv_acc[slot, 0] += d_k
            kv_acc[slot, 1] += d_v

    def finish(kt, slot):
        @pl.when(jnp.logical_and(kt % 2 == core, kt <= last_chunk))
        def _():
            sib_copy(kt // 2).wait_recv()
            for which, scale in ((0, SCALE), (1, 1.0)):
                both = kv_acc[slot, which] * scale + sibb[kt // 2, which].astype(F32)
                dkvs[kt // 2, :, which] = both.astype(BF16).reshape(4, HEAD, HEAD)
            loop((kt // 2) * 4 + 4, lambda i: send(*dkv_plan(i)), (kt // 2) * 4)

    first = hl0 + 2 * y

    def key_chunk(t, _):
        kt, slot = (first + t) % 8, t % 2
        for qc in (1, 0):
            @pl.when(kt <= chunks[qc])
            def _():
                backward(qc, kt, slot)

        @pl.when(jnp.logical_and(kt % 2 != core, kt <= 7 - r0))
        def _():
            for which, scale in ((0, SCALE), (1, 1.0)):
                sibs[kt // 2, which] = (kv_acc[slot, which] * scale).astype(BF16)
            sib_copy(kt // 2).start()

        @pl.when(jnp.logical_and(kt % 2 == core, kt > 7 - r0))
        def _():
            kv_acc[slot] = jnp.zeros((2, CHUNK, HEAD), F32)

        @pl.when(t > 0)
        def _():
            finish((kt + 7) % 8, 1 - slot)

        return 0

    lax.fori_loop(0, 4, key_chunk, 0)
    arrived(ob, o_recv)
    arrived(hst, h_recv)
    square_row = hst[0, pl.ds(own_slot, 1), :]
    rstd_row = lax.rsqrt(square_row / WIDTH + EPS)
    rstd = jnp.broadcast_to(rstd_row, (BLOCK, BLOCK)).T
    for hl in range(8):
        cols = slice(hl * HEAD, (hl + 1) * HEAD)
        a_hat = ob[hl].astype(F32) * rstd
        normed = a_hat * gain[:, cols]
        gate = gi_ref[:, cols].astype(F32)
        zx[pl.ds(8, BLOCK), cols] = gate * normed
        ggi_ref[:, cols] = (dz[:, cols] * normed).astype(BF16)
        g_near[z * 4 + y, 1, hl : hl + 1, :] = jnp.sum(dz[:, cols] * gate * a_hat, axis=0, keepdims=True)

    @pl.when(p < 31)
    def _():
        z_rim.start()

    @pl.when(p == 0)
    def _():
        zx[pl.ds(0, 8), :] = jnp.zeros((8, 1024), F32)

    lax.fori_loop(4, 6, key_chunk, 0)
    @pl.when(p > 0)
    def _():
        z_rim.wait_recv()

    tap_sums = []
    for hl in range(8):
        cols = slice(hl * HEAD, (hl + 1) * HEAD)
        d_conv = du[pl.ds(0, BLOCK), cols]
        conv = jnp.zeros((BLOCK, HEAD), F32)
        sums = []
        for lag in range(FILT):
            shifted = zx[pl.ds(8 - lag, BLOCK), cols]
            conv = conv + taps[lag : lag + 1, cols] * shifted
            sums.append(jnp.sum(d_conv * shifted, axis=0, keepdims=True))
        sums.append(jnp.zeros((1, HEAD), F32))
        tap_sums.append(jnp.concatenate(sums, axis=0))
        mixed_ref[:, cols] = (go_ref[:, cols].astype(F32) * conv).astype(BF16)
        ggo_ref[:, cols] = (cot_ref[:, cols].astype(F32) * conv).astype(BF16)
    g_near[z * 4 + y, 0] = dot(jnp.concatenate(tap_sums, axis=1), spread, 1, 1, lax.Precision.HIGHEST)
    each(g_plan, 8, send, 1)
    lax.fori_loop(6, 8, key_chunk, 0)
    finish((first + 7) % 8, 1)
    for qc in range(2):
        dq = dq_acc[:, qc * CHUNK : (qc + 1) * CHUNK] * SCALE
        dqs[pl.ds(qc * 4, 4)] = dq.T.astype(BF16).reshape(4, HEAD, HEAD)
    each(dq_plan, 8, send)
    arrived(g_near.at[pl.ds(0, 7)], g_recv)
    g_far[x] = jnp.sum(g_near[...], axis=0)
    each(gx_plan, 4, send, 1)
    each(o_plan, 8, sent)
    sent(*h_args)
    each(su_plan, 8, sent, 1)
    each(g_plan, 8, sent, 1)
    arrived(g_far.at[pl.ds(0, 3)], gx_recv)
    g_total = jnp.sum(g_far[...], axis=0)
    gf_ref[...] = g_total[0, :FILT]
    gg_ref[...] = g_total[1]
    loop(16, lambda i: kv_wanted(i, sent))
    each(q_plan, 8, sent)
    loop(16, lambda i: relay_wanted(i, lambda *a: sent(*a[:6])))
    each(st_plan, 4, sent, 1)
    each(s_plan, 8, sent)
    lax.fori_loop(0, 4, lambda i, _: (sib_sent(i), 0)[1], 0)
    lax.fori_loop(0, 16, lambda i, _: (dkv_sent(i), 0)[1], 0)
    each(dq_plan, 8, sent)
    each(gx_plan, 4, sent, 1)

    @pl.when(p > 0)
    def _():
        du_rim.wait_send()

    @pl.when(p < 31)
    def _():
        z_rim.wait_send()

    arrived(dqb, dq_recv)

    def all_keys(parts):
        arrived(dkvb.at[pl.ds(0, parts * 8)], dkv_recv)
        for hl in range(8):
            cols = slice(hl * HEAD, (hl + 1) * HEAD)
            for which, out_ref in ((0, gk_ref), (1, gv_ref)):
                total = dkvb[hl, which]
                if parts == 2:
                    total = (total.astype(F32) + dkvb[8 + hl, which].astype(F32)).astype(BF16)
                out_ref[:, cols] = total

    for hl in range(8):
        gq_ref[:, hl * HEAD : (hl + 1) * HEAD] = dqb[hl]

    @pl.when(own_chunk <= 5)
    def _():
        all_keys(2)

    @pl.when(own_chunk > 5)
    def _():
        all_keys(1)


def handed_on(*refs):
    held, in_sem, out_sem = refs[16:24], refs[24], refs[25]
    loads = [pltpu.make_async_copy(refs[i], held[i], in_sem.at[i]) for i in range(8)]
    stores = [pltpu.make_async_copy(held[i], refs[8 + i], out_sem.at[i]) for i in range(8)]
    for load in loads:
        load.start()
    for load, store in zip(loads, stores):
        load.wait()
        store.start()
    for store in stores:
        store.wait()


def shards(queries, key_rows, value_rows, gate_in, gate_out, kernel_taps, norm_gain, cotangent):
    rows = jax.ShapeDtypeStruct((BLOCK, 1024), BF16)
    vmem = pl.BlockSpec(memory_space=pltpu.VMEM)
    hbm = pl.BlockSpec(memory_space=pl.ANY)
    tile = (HEAD, HEAD)
    dma = pltpu.SemaphoreType.DMA
    outs = pl.pallas_call(
        kernel,
        out_shape=[rows] * 6 + [jax.ShapeDtypeStruct((FILT, 128), F32), jax.ShapeDtypeStruct((8, 128), F32)],
        in_specs=[hbm] * 5 + [vmem] * 2 + [hbm],
        out_specs=[vmem] * 8,
        scratch_shapes=[
            pltpu.VMEM((8, 2, *tile), BF16),
            pltpu.VMEM((8, *tile), BF16),
            pltpu.VMEM((8, *tile), BF16),
            pltpu.VMEM((32, 2, *tile), BF16),
            pltpu.VMEM((8, *tile), BF16),
            pltpu.VMEM((8, *tile), BF16),
            pltpu.VMEM((BLOCK + 8, 1024), F32),
            pltpu.VMEM((BLOCK, 1024), F32),
            pltpu.VMEM((HEAD, 1024), F32),
            pltpu.VMEM((1, 1024), F32),
            pltpu.VMEM((8, *tile), BF16),
            pltpu.VMEM((8, *tile), BF16),
            pltpu.VMEM((4, 2, 8, 128), F32),
            pltpu.VMEM((8, 2, 8, 128), F32),
            pltpu.VMEM((2, 8, 128), F32),
            pltpu.VMEM((2, 8, 128), F32),
            pltpu.VMEM((8, *tile), BF16),
            pltpu.VMEM((8, *tile), BF16),
            pltpu.VMEM((1, 1024), F32),
            pltpu.VMEM((1, 1024), F32),
            pltpu.VMEM((HEAD, 1024), F32),
            pltpu.VMEM((HEAD, 1024), F32),
            pltpu.VMEM((HEAD, 1024), BF16),
            pltpu.VMEM((1024, HEAD), BF16),
            pltpu.VMEM((1, 1024), F32),
            pltpu.VMEM((2, 2, CHUNK, HEAD), F32),
            pltpu.VMEM((4, 2, CHUNK, HEAD), BF16),
            pltpu.VMEM((4, 2, CHUNK, HEAD), BF16),
            pltpu.VMEM((4, 4, 2, *tile), BF16),
            pltpu.VMEM((16, 2, *tile), BF16),
            pltpu.VMEM((BLOCK + 8, 1024), F32),
            pltpu.VMEM((8, 2, 8, 128), F32),
            pltpu.VMEM((4, 2, 8, 128), F32),
            pltpu.VMEM((BLOCK, 1024), BF16),
            pltpu.VMEM((BLOCK, 1024), BF16),
            pltpu.VMEM((BLOCK, 1024), BF16),
            pltpu.VMEM((16, CHUNK, CHUNK), BF16),
            pltpu.VMEM((16, 1, CHUNK), F32),
            dma((8,)), dma, dma((4,)), dma,
            dma((5,)),
            dma((16,)), dma, dma((4,)), dma((4,)),
            dma((16,)), dma((8,)), dma((8,)), dma((8,)), dma((4,)), dma, dma((8,)), dma((16,)), dma((8,)),
            dma((2,)),
            dma((16,)), dma, dma, dma, dma, dma, dma, dma, dma, dma((2,)),
        ],
        compiler_params=pltpu.CompilerParams(collective_id=0, has_side_effects=True, vmem_limit_bytes=56 * 1024 * 1024),
        name="hyena",
    )(
        queries, key_rows, value_rows, gate_in, gate_out, kernel_taps.T, norm_gain.reshape(1, -1), cotangent
    )
    mixed, gq, gk, gv, ggi, ggo, gf, gg = pl.pallas_call(
        handed_on,
        out_shape=[jax.ShapeDtypeStruct(o.shape, o.dtype) for o in outs],
        in_specs=[hbm] * 8,
        out_specs=[hbm] * 8,
        scratch_shapes=[pltpu.VMEM(o.shape, o.dtype) for o in outs] + [dma((8,)), dma((8,))],
        name="results",
    )(*outs)
    return mixed, gq, gk, gv, ggi, ggo, gf.T, gg.reshape(-1)


def solution(mesh):
    wide = P("ctx", "chan")
    thin = (P("chan", None), P("chan"))
    return jax.shard_map(
        shards, mesh=mesh, in_specs=(wide,) * 5 + thin + (wide,), out_specs=(wide,) * 6 + thin, check_vma=False
    )
```
